32 devices in a mesh: groups: 2 (over y), ctx: 4 (over z), section: 2 (over x), head: 2 (over core).
Axes of the slice: x: 2, y: 2, z: 4, core: 2. Of those that a mesh axis runs over, the one named last changes fastest.
Arguments:
- queries: bfloat16 [2, 2, 2048, 3584], P('section', None, ('groups', 'ctx'), 'head'), parts along dimension 2, may hold values from -120 to 120
- key_row_table: bfloat16 [2, 2, 2048, 512], P('section', None, ('groups', 'ctx'), 'head'), parts along dimension 2, may hold values from -7 to 7
- value_row_table: bfloat16 [2, 2, 2048, 512], P('section', None, ('groups', 'ctx'), 'head'), parts along dimension 2, may hold values from -6 to 6
- vertical_cols: int32 [2, 4, 2048], P('section', 'head', 'groups'), parts along dimension 2, may hold values from 0 to 2047, as said below
- slash_offsets: int32 [2, 28, 128], P('section', 'head', 'groups'), parts along dimension 2, may hold values from 0 to 255, as said below
Outputs:
- attended: bfloat16 [2, 2, 2048, 3584], P('section', None, ('groups', 'ctx'), 'head'), parts along dimension 2
The draws below stay inside these ranges and needn't reach their ends.
There are 2 independent parts, one for each index of `groups`. The reference program is written for one: setup_inputs(seed, part) draws one part's arguments, and reference() takes and returns one part's arrays. A program takes and returns all parts, laid end to end along the dimension named above; each array names one. Nothing has to cross between parts.
Inputs may be any that keep to these rules, and one draw needn't show every extreme that they name: `vertical_cols`: each run of 128 entries of a kv head's list (a tile) holds positions of one rank's rows of one micro-half; a kv head's positions are distinct; at most 2 tiles of a kv head lie on one rank, and for every kv head some rank holds exactly 2. `slash_offsets`: each head's offsets are distinct and include 0 and 255.
All inputs are finite; a program needn't handle non-finite values.
Results may differ from the reference program's by a relative error of at most 0.0032.
Values may be sent and summed in bfloat16 or wider, within the bound.
No kernel may reach another device: no remote copies, remote signals or barrier semaphores. Data moves between devices by JAX's collectives and lax.ppermute only.
A program may use at most 64 MiB of HBM per device.

```python
import jax
import jax.numpy as jnp
from jax import lax

HQ = 28
KEY_VALUE_HEADS = 4
HEAD_SIZE = 128
QUERY_PER_KV = 7
ROWS = 256
TILE_COLUMNS = 128
VERTICAL_TILES = 8
MAXT = 2
NS = 64
LAYER_COUNT = 2
TOKENS_PER_HALF = 1024


def shared_base(key):
    drawn_result = jax.random.normal(key, (LAYER_COUNT, 2, TOKENS_PER_HALF, KEY_VALUE_HEADS * HEAD_SIZE), jnp.float32)
    return jnp.clip(drawn_result, -5.0, 5.0)


def draw_key_row_table(key, part):
    base_offset = shared_base(key)
    return (1.4 * base_offset).astype(jnp.bfloat16)


def draw_queries(key, part):
    key = jax.random.fold_in(key, 2)
    fresh = jnp.clip(jax.random.normal(key, (LAYER_COUNT, 2, TOKENS_PER_HALF, HQ * HEAD_SIZE), jnp.float32), -5.0, 5.0)
    result = 1.4 * fresh
    return result.astype(jnp.bfloat16)


def span_permutation(span_key):
    return jax.random.permutation(span_key, ROWS)


def slot_permutation(slot_key):
    return jax.random.permutation(slot_key, 2 * (ROWS // TILE_COLUMNS))


def single_head_tiles(sub_key):
    rank_total = TOKENS_PER_HALF // ROWS
    per_span = ROWS // TILE_COLUMNS
    groups_used = (VERTICAL_TILES + MAXT - 1) // MAXT
    parts = jax.random.split(sub_key, 4)
    rank_order = jax.random.permutation(parts[0], rank_total)[:groups_used].astype(jnp.int32)
    tile_ids = jnp.arange(VERTICAL_TILES, dtype=jnp.int32)
    owners = rank_order[tile_ids // MAXT]
    slot_perm = jax.vmap(slot_permutation)(jax.random.split(parts[1], groups_used)).astype(jnp.int32)
    slot_ids = slot_perm[tile_ids // MAXT, tile_ids % MAXT]
    shuffle = jax.random.permutation(parts[2], VERTICAL_TILES)
    owners = owners[shuffle]
    slot_ids = slot_ids[shuffle]
    half_ids = slot_ids // per_span
    piece_ids = slot_ids % per_span
    span_keys = jax.random.split(parts[3], 2 * rank_total)
    perms = jax.vmap(span_permutation)(span_keys).reshape(2, rank_total, ROWS)
    span_perm = perms[half_ids, owners]
    within = jnp.take_along_axis(span_perm, piece_ids[:, None] * TILE_COLUMNS + jnp.arange(TILE_COLUMNS, dtype=jnp.int32)[None, :], axis=1)
    span_start = half_ids * TOKENS_PER_HALF + owners * ROWS
    return (span_start[:, None] + within).reshape(VERTICAL_TILES * TILE_COLUMNS).astype(jnp.int32)


def draw_vertical_cols(key, part):
    key = jax.random.fold_in(key, 3)
    derived_keys = jax.random.split(key, LAYER_COUNT * KEY_VALUE_HEADS)
    return jax.vmap(single_head_tiles)(derived_keys).reshape(LAYER_COUNT, KEY_VALUE_HEADS, VERTICAL_TILES * TILE_COLUMNS)


def one_head_offsets(sub_key):
    parts = jax.random.split(sub_key, 2)
    others = jax.random.permutation(parts[0], ROWS - 2)[:NS - 2] + 1
    fixed_ends = jnp.array([0, ROWS - 1], jnp.int32)
    values_all = jnp.concatenate([fixed_ends, others.astype(jnp.int32)])
    return values_all[jax.random.permutation(parts[1], NS)]


def draw_slash_offsets(key, part):
    key = jax.random.fold_in(key, 4)
    derived_keys = jax.random.split(key, LAYER_COUNT * HQ)
    return jax.vmap(one_head_offsets)(derived_keys).reshape(LAYER_COUNT, HQ, NS)


def shard_levels(key, shape, pieces, least, largest):
    level = 1.0
    for dim, blocks in pieces:
        heights = jax.random.uniform(jax.random.fold_in(jax.random.fold_in(key, 6), dim), (blocks,), jnp.float32, least / len(pieces), largest / len(pieces))
        level = level * jnp.repeat(jnp.exp(heights), shape[dim] // blocks).reshape((-1,) + (1,) * (len(shape) - 1 - dim))
    return level


def gaussian(stream_key, dims, width, most, pieces=(), kind=jnp.bfloat16):
    gain = shard_levels(stream_key, dims, pieces, -0.22, 0.18) if pieces else 1.0
    drawn = jax.random.normal(stream_key, dims, jnp.float32) * width * gain
    return jnp.minimum(jnp.maximum(drawn, -most), most).astype(kind)


def setup_inputs(seed: int = 0, part: int = 0) -> dict:
    splits = jax.random.split(jax.random.key(seed), 6)
    own_keys = jax.random.split(jax.random.fold_in(splits[5], part), 6)
    return {
        "queries": draw_queries(jax.random.fold_in(jax.random.fold_in(splits[5], part), 71), part),
        "key_row_table": draw_key_row_table(jax.random.fold_in(jax.random.fold_in(splits[5], part), 71), part),
        "value_row_table": gaussian(own_keys[2], (LAYER_COUNT, 2, TOKENS_PER_HALF, KEY_VALUE_HEADS * HEAD_SIZE), 1.0, 6.0, ((0, 2), (2, 4), (3, 2))),
        "vertical_cols": draw_vertical_cols(jax.random.fold_in(jax.random.fold_in(splits[5], part), 71), part),
        "slash_offsets": draw_slash_offsets(jax.random.fold_in(jax.random.fold_in(splits[5], part), 71), part),
    }


def reference(queries, key_row_table, value_row_table, vertical_cols, slash_offsets):
    prompt_length = 2 * TOKENS_PER_HALF
    block_rows = 2 * ROWS
    scaling = 1.0 / (HEAD_SIZE ** 0.5)
    layers_out = []
    for layer_number in range(LAYER_COUNT):
        query_all = queries[layer_number].reshape(prompt_length, HQ, HEAD_SIZE)
        key_gathered = key_row_table[layer_number].reshape(prompt_length, KEY_VALUE_HEADS, HEAD_SIZE)
        value_gathered = value_row_table[layer_number].reshape(prompt_length, KEY_VALUE_HEADS, HEAD_SIZE)
        cols_layer = vertical_cols[layer_number]
        offsets_layer = slash_offsets[layer_number]

        def per_head(head_id):
            group_id = head_id // QUERY_PER_KV
            query_head = lax.dynamic_index_in_dim(query_all, head_id, 1, keepdims=False)
            key_head = lax.dynamic_index_in_dim(key_gathered, group_id, 1, keepdims=False)
            value_head = lax.dynamic_index_in_dim(value_gathered, group_id, 1, keepdims=False)
            columns = lax.dynamic_index_in_dim(cols_layer, group_id, 0, keepdims=False)
            offsets = lax.dynamic_index_in_dim(offsets_layer, head_id, 0, keepdims=False)
            marked = jnp.zeros((prompt_length,), jnp.int32).at[columns].set(1)
            key_vert = key_head[columns]
            value_vert = value_head[columns]

            def per_block(block_id):
                first_row = block_id * block_rows
                query_block = lax.dynamic_slice_in_dim(query_head, first_row, block_rows, 0)
                position = first_row + jnp.arange(block_rows, dtype=jnp.int32)
                score_vert = jnp.dot(query_block, key_vert.T, preferred_element_type=jnp.float32) * scaling
                live_vert = columns[None, :] <= position[:, None]
                source = position[:, None] - offsets[None, :]
                clipped = jnp.clip(source, 0, prompt_length - 1)
                live_band = (source >= 0) & (marked[clipped] == 0)
                key_band = key_head[clipped].astype(jnp.float32)
                value_band = value_head[clipped].astype(jnp.float32)
                score_band = jnp.einsum("bd,bsd->bs", query_block.astype(jnp.float32), key_band) * scaling
                row_max = jnp.maximum(
                    jnp.max(jnp.where(live_vert, score_vert, -jnp.inf), axis=1),
                    jnp.max(jnp.where(live_band, score_band, -jnp.inf), axis=1))
                expo_vert = jnp.exp(jnp.where(live_vert, score_vert - row_max[:, None], -jnp.inf))
                expo_band = jnp.exp(jnp.where(live_band, score_band - row_max[:, None], -jnp.inf))
                weight_sum = jnp.sum(expo_vert, axis=1) + jnp.sum(expo_band, axis=1)
                weights_vert = expo_vert.astype(jnp.bfloat16)
                weights_band = expo_band.astype(jnp.bfloat16)
                weighted = jnp.dot(weights_vert, value_vert, preferred_element_type=jnp.float32)
                weighted = weighted + jnp.einsum("bs,bsd->bd", weights_band.astype(jnp.float32), value_band)
                return (weighted / weight_sum[:, None]).astype(jnp.bfloat16)

            blocks_out = lax.map(per_block, jnp.arange(prompt_length // block_rows, dtype=jnp.int32))
            return blocks_out.reshape(prompt_length, HEAD_SIZE)

        heads_out = lax.map(per_head, jnp.arange(HQ, dtype=jnp.int32))
        layers_out.append(heads_out.transpose(1, 0, 2).reshape(2, TOKENS_PER_HALF, HQ * HEAD_SIZE))
    return jnp.stack(layers_out)
```

```python
import functools
import math

import jax
import jax.numpy as jnp
from jax import lax
from jax.experimental import pallas as pl
from jax.experimental.pallas import tpu as pltpu
from jax.sharding import PartitionSpec as P

HEAD_SIZE = 128
TILE_COLUMNS = 128
MAXT = 2
DEAD = -1e30
SCALE2 = math.log2(math.e) / math.sqrt(HEAD_SIZE)
VMEM_BYTES = 48 * 1024 * 1024


def dot_nt(a, b):
    return lax.dot_general(a, b, (((1,), (1,)), ((), ())), preferred_element_type=jnp.float32)


def dot_nn(a, b):
    return lax.dot_general(a, b, (((1,), (0,)), ((), ())), preferred_element_type=jnp.float32)


def prep_kernel(n, rows, kv, rank_ref, cols_smem, cols_ref, k_ref, v_ref, *outs):
    pack0_ref, pack1_ref = outs[:2]
    payload_refs = outs[2 : 2 + n - 2]
    band_bias_ref, extra_bias_ref, remote_bias_ref = outs[2 + n - 2 : 5 + n - 2]
    outbox_ref, marks_ref, slot_ref, count_ref = outs[5 + n - 2 :]
    rank = rank_ref[0]
    half_len = rows * n
    tiles = cols_ref.shape[1] // TILE_COLUMNS
    per_rank = rows // TILE_COLUMNS
    pack0_ref[0] = k_ref[0]
    pack0_ref[1] = v_ref[0]
    pack1_ref[0] = k_ref[1]
    pack1_ref[1] = v_ref[1]

    for g in range(kv):
        for s in range(n):
            count_ref[g, s] = 0
            for slot in range(MAXT):
                slot_ref[g, s * MAXT + slot] = -1
        for t in range(tiles):
            owner = cols_smem[g, t * TILE_COLUMNS] % half_len // rows
            seen = count_ref[g, owner]
            slot_ref[g, owner * MAXT + seen] = t
            count_ref[g, owner] = seen + 1

    for g in range(kv):
        lanes = slice(g * HEAD_SIZE, (g + 1) * HEAD_SIZE)
        for slot in range(MAXT):
            tile = jnp.maximum(slot_ref[g, rank * MAXT + slot], 0)
            start = pl.multiple_of(tile * TILE_COLUMNS, TILE_COLUMNS)
            half = cols_smem[g, start] // half_len
            within = cols_ref[pl.ds(g, 1), pl.ds(start, TILE_COLUMNS)] % rows
            hit = lax.broadcasted_iota(jnp.int32, (rows, TILE_COLUMNS), 0) == within
            pick = jnp.where(hit, 1.0, 0.0).astype(jnp.bfloat16)
            for which, ref in enumerate((k_ref, v_ref)):
                source = ref[pl.ds(half, 1), :, lanes][0]
                got = lax.dot_general(
                    pick, source, (((0,), (0,)), ((), ())), preferred_element_type=jnp.float32
                )
                outbox_ref[which, slot * TILE_COLUMNS : (slot + 1) * TILE_COLUMNS, lanes] = (
                    got.astype(jnp.bfloat16)
                )
    for i, ref in enumerate(payload_refs):
        d = i + 2

        @pl.when(rank + d < n)
        def _():
            ref[...] = outbox_ref[...]

        @pl.when(rank + d >= n)
        def _():
            ref[0] = k_ref[0]
            ref[1] = v_ref[0]

    blocks = 2 * n * per_rank
    dead_row = jnp.full((1, rows), DEAD, jnp.float32)
    for g in range(kv):
        cols = cols_ref[g : g + 1, :]
        high = lax.broadcasted_iota(jnp.int32, (blocks, cols.shape[1]), 0) == cols // TILE_COLUMNS
        low = lax.broadcasted_iota(jnp.int32, (TILE_COLUMNS, cols.shape[1]), 0) == cols % TILE_COLUMNS
        count = dot_nt(
            jnp.where(high, 1.0, 0.0).astype(jnp.bfloat16),
            jnp.where(low, 1.0, 0.0).astype(jnp.bfloat16),
        )
        marks_ref[g] = jnp.where(count > 0.5, 0.0, DEAD)

        def marks_of(half, s):
            first = (half * n + s) * per_rank
            return jnp.concatenate(
                [marks_ref[g, pl.ds(first + i, 1), :] for i in range(per_rank)], axis=1
            )

        first_rank = rank == 0
        before = jnp.where(first_rank, n - 1, rank - 1)
        before_low = marks_of(0, before)
        own_low = marks_of(0, rank)
        own_high = marks_of(1, rank)
        before_high = marks_of(jnp.where(first_rank, 0, 1), before)
        band_bias_ref[g, 0:1, :rows] = jnp.where(first_rank, dead_row, before_low)
        band_bias_ref[g, 0:1, rows:] = own_low
        band_bias_ref[g, 1:2, :rows] = before_high
        band_bias_ref[g, 1:2, rows:] = own_high
        extra_bias_ref[g, 0:1, :rows] = own_low
        extra_bias_ref[g, 0:1, rows:] = jnp.where(first_rank, dead_row, before_low)
        for i in range(n - 2):
            d = i + 2
            earlier = rank >= d
            s = jnp.where(earlier, rank - d, rank - d + n)
            raw = marks_of(0, s)
            for slot in range(MAXT):
                tile = slot_ref[g, s * MAXT + slot]
                half = cols_smem[g, jnp.maximum(tile, 0) * TILE_COLUMNS] // half_len
                live = tile >= 0
                high_value = jnp.where(live, 0.0, DEAD)
                low_value = jnp.where(live & (half == 0) & earlier, 0.0, DEAD)
                span = slice(i * rows + slot * TILE_COLUMNS, i * rows + (slot + 1) * TILE_COLUMNS)
                part = slice(slot * TILE_COLUMNS, (slot + 1) * TILE_COLUMNS)
                remote_bias_ref[g, 0:1, span] = jnp.full((1, TILE_COLUMNS), low_value, jnp.float32)
                remote_bias_ref[g, 1:2, span] = jnp.where(
                    earlier, jnp.full((1, TILE_COLUMNS), high_value, jnp.float32), raw[:, part]
                )


def near_kernel(
    rows, kv, group_size,
    rank_ref, q_ref, k_ref, v_ref, in0_ref, in1_ref, band_bias_ref, extra_bias_ref, slash_ref,
    acc_ref, stat_ref,
    kb_ref, vb_ref, kx_ref, vx_ref, tri_ref,
):
    first_rank = rank_ref[0] == 0
    t = rows // 2
    tri = lax.broadcasted_iota(jnp.int32, (t, t), 0) >= lax.broadcasted_iota(jnp.int32, (t, t), 1)
    ones = jnp.ones((2 * rows, HEAD_SIZE), jnp.bfloat16)
    for g in range(kv):
        lanes = slice(g * HEAD_SIZE, (g + 1) * HEAD_SIZE)
        for which, own, band, extra in ((0, k_ref, kb_ref, kx_ref), (1, v_ref, vb_ref, vx_ref)):
            low = in0_ref[which, :, lanes]
            high = in1_ref[which, :, lanes]
            band[g, 0, :rows, :HEAD_SIZE] = low
            band[g, 0, rows:, :HEAD_SIZE] = own[0, :, lanes]
            band[g, 1, :rows, :HEAD_SIZE] = jnp.where(first_rank, low, high)
            band[g, 1, rows:, :HEAD_SIZE] = own[1, :, lanes]
            extra[g, :rows, :HEAD_SIZE] = own[0, :, lanes]
            extra[g, rows:, :HEAD_SIZE] = low
        for m in range(2):
            vb_ref[g, m, :, HEAD_SIZE:] = ones
            for b in range(2):
                row = band_bias_ref[g, m : m + 1, rows + b * t : rows + (b + 1) * t]
                tri_ref[g, m, b] = jnp.where(tri, row, DEAD)
        vx_ref[g, :, HEAD_SIZE:] = ones
    shut = jnp.where(first_rank, DEAD, 0.0)
    lane = lax.broadcasted_iota(jnp.int32, (rows, HEAD_SIZE), 1)

    for g in range(kv):

        def one_head(h, carry):
            head = g * group_size + h
            at = pl.ds(pl.multiple_of(head * HEAD_SIZE, HEAD_SIZE), HEAD_SIZE)
            base = jnp.broadcast_to(slash_ref[head], (t, 2 * rows))
            rolled = pltpu.roll(base, 1, 1, stride=1, stride_axis=0)
            t2, t1, t0 = rolled[:, :t], rolled[:, t : 2 * t], rolled[:, 2 * t : 3 * t]
            for m in range(2):
                q = q_ref[m, :, at]
                s = dot_nt(q, kb_ref[g, m]) * SCALE2
                p2, p1 = (t2 + shut, t1 + shut) if m == 0 else (t2, t1)
                row = [band_bias_ref[g, m : m + 1, b * t : (b + 1) * t] for b in range(4)]
                top = [
                    s[:t, :t] + jnp.maximum(p2, row[0]),
                    s[:t, t : 2 * t] + jnp.maximum(p1, row[1]),
                    s[:t, 2 * t : 3 * t] + jnp.maximum(t0, tri_ref[g, m, 0]),
                ]
                low = [
                    s[t:, :t] + row[0],
                    s[t:, t : 2 * t] + jnp.maximum(p2, row[1]),
                    s[t:, 2 * t : 3 * t] + jnp.maximum(t1, row[2]),
                    s[t:, 3 * t :] + jnp.maximum(t0, tri_ref[g, m, 1]),
                ]
                top_max = functools.reduce(jnp.maximum, top)
                low_max = functools.reduce(jnp.maximum, low)
                all_max = jnp.concatenate([top_max, low_max], axis=0)
                if m == 1:
                    sx = dot_nt(q, kx_ref[g]) * SCALE2 + extra_bias_ref[g]
                    for b in range(4):
                        all_max = jnp.maximum(all_max, sx[:, b * t : (b + 1) * t])
                peak = jnp.max(all_max, axis=1, keepdims=True)
                top = [jnp.exp2(x - peak[:t]).astype(jnp.bfloat16) for x in top]
                top.append(jnp.zeros((t, t), jnp.bfloat16))
                low = [jnp.exp2(x - peak[t:]).astype(jnp.bfloat16) for x in low]
                p = jnp.concatenate(
                    [jnp.concatenate(top, axis=1), jnp.concatenate(low, axis=1)], axis=0
                )
                o = dot_nn(p, vb_ref[g, m])
                if m == 1:
                    px = jnp.exp2(sx - peak).astype(jnp.bfloat16)
                    o = o + dot_nn(px, vx_ref[g])
                acc_ref[m, :, at] = o[:, :HEAD_SIZE]
                stat_ref[m, :, at] = jnp.where(lane < HEAD_SIZE // 2, peak, o[:, HEAD_SIZE:])
            return carry

        lax.fori_loop(0, group_size, one_head, 0)


def far_kernel(rows, kv, group_size, count, *refs):
    q_ref, acc_ref, stat_ref, remote_bias_ref = refs[:4]
    arrived = refs[4 : 4 + count]
    out_ref, kr_ref, vr_ref = refs[4 + count :]
    ones = jnp.ones((rows, HEAD_SIZE), jnp.bfloat16)
    for g in range(kv):
        lanes = slice(g * HEAD_SIZE, (g + 1) * HEAD_SIZE)
        for i, ref in enumerate(arrived):
            at = slice(i * rows, (i + 1) * rows)
            kr_ref[g, at, :] = ref[0, :, lanes]
            vr_ref[g, at, :HEAD_SIZE] = ref[1, :, lanes]
            vr_ref[g, at, HEAD_SIZE:] = ones

    for g in range(kv):

        def one_head(h, carry):
            head = g * group_size + h
            at = pl.ds(pl.multiple_of(head * HEAD_SIZE, HEAD_SIZE), HEAD_SIZE)
            for m in range(2):
                q = q_ref[m, :, at]
                s = dot_nt(q, kr_ref[g]) * SCALE2 + remote_bias_ref[g, m : m + 1, :]
                stat = stat_ref[m, :, at]
                old = stat[:, :1]
                peak = jnp.maximum(old, jnp.max(s, axis=1, keepdims=True))
                p = jnp.exp2(s - peak).astype(jnp.bfloat16)
                o = dot_nn(p, vr_ref[g])
                shrink = jnp.exp2(old - peak)
                total = stat[:, HEAD_SIZE - 1 :] * shrink + o[:, HEAD_SIZE:]
                out = (acc_ref[m, :, at] * shrink + o[:, :HEAD_SIZE]) / total
                out_ref[m, :, at] = out.astype(jnp.bfloat16)
            return carry

        lax.fori_loop(0, group_size, one_head, 0)


def per_device(queries, key_row_table, value_row_table, vertical_cols, slash_offsets):
    n = lax.axis_size("ctx")
    rank = lax.axis_index("ctx").astype(jnp.int32)
    rows = queries.shape[2]
    kv = key_row_table.shape[3] // HEAD_SIZE
    heads = queries.shape[3] // HEAD_SIZE
    group_size = heads // kv
    q, k, v = queries[0], key_row_table[0], value_row_table[0]
    cols = vertical_cols[0]
    count = n - 2
    per_rank = rows // TILE_COLUMNS
    vmem = pl.BlockSpec(memory_space=pltpu.VMEM)
    smem = pl.BlockSpec(memory_space=pltpu.SMEM)
    params = pltpu.CompilerParams(vmem_limit_bytes=VMEM_BYTES)
    unit = jax.ShapeDtypeStruct((2, rows, kv * HEAD_SIZE), jnp.bfloat16)
    rank1 = rank[None]

    prepared = pl.pallas_call(
        functools.partial(prep_kernel, n, rows, kv),
        out_shape=[unit] * (2 + count)
        + [
            jax.ShapeDtypeStruct((kv, 2, 2 * rows), jnp.float32),
            jax.ShapeDtypeStruct((kv, 1, 2 * rows), jnp.float32),
            jax.ShapeDtypeStruct((kv, 2, count * rows), jnp.float32),
        ],
        in_specs=[smem, smem, vmem, vmem, vmem],
        out_specs=[vmem] * (5 + count),
        scratch_shapes=[
            pltpu.VMEM((2, rows, kv * HEAD_SIZE), jnp.bfloat16),
            pltpu.VMEM((kv, 2 * n * per_rank, TILE_COLUMNS), jnp.float32),
            pltpu.SMEM((kv, n * MAXT), jnp.int32),
            pltpu.SMEM((kv, n), jnp.int32),
        ],
        compiler_params=params,
        name="prep",
    )(rank1, cols, cols, k, v)
    pack0, pack1 = prepared[:2]
    payloads = prepared[2 : 2 + count]
    band_bias, extra_bias, remote_bias = prepared[2 + count :]

    def shifted(x, d):
        return lax.ppermute(x, "ctx", [(i, (i + d) % n) for i in range(n)])

    in0 = shifted(pack0, 1)
    in1 = lax.ppermute(pack1, "ctx", [(i, i + 1) for i in range(n - 1)])
    arrived = [shifted(x, i + 2) for i, x in enumerate(payloads)]

    reach = rows - 1 - jnp.arange(2 * rows, dtype=jnp.int32)
    hit = jnp.any(slash_offsets[0][:, :, None] == reach[None, None, :], axis=1)
    slash = jnp.where(hit, 0.0, DEAD).astype(jnp.float32)[:, None, :]

    state = jax.ShapeDtypeStruct((2, rows, heads * HEAD_SIZE), jnp.float32)
    acc, stat = pl.pallas_call(
        functools.partial(near_kernel, rows, kv, group_size),
        out_shape=[state, state],
        in_specs=[smem] + [vmem] * 8,
        out_specs=[vmem] * 2,
        scratch_shapes=[
            pltpu.VMEM((kv, 2, 2 * rows, HEAD_SIZE), jnp.bfloat16),
            pltpu.VMEM((kv, 2, 2 * rows, 2 * HEAD_SIZE), jnp.bfloat16),
            pltpu.VMEM((kv, 2 * rows, HEAD_SIZE), jnp.bfloat16),
            pltpu.VMEM((kv, 2 * rows, 2 * HEAD_SIZE), jnp.bfloat16),
            pltpu.VMEM((kv, 2, 2, rows // 2, rows // 2), jnp.float32),
        ],
        compiler_params=params,
        cost_estimate=pl.CostEstimate(
            flops=heads * 2 * rows * 6 * rows * HEAD_SIZE * 4, bytes_accessed=16_000_000,
            transcendentals=heads * 6 * rows * rows,
        ),
        name="near",
    )(rank1, q, k, v, in0, in1, band_bias, extra_bias, slash)

    out = pl.pallas_call(
        functools.partial(far_kernel, rows, kv, group_size, count),
        out_shape=jax.ShapeDtypeStruct(q.shape, jnp.bfloat16),
        in_specs=[vmem] * (4 + count),
        out_specs=vmem,
        scratch_shapes=[
            pltpu.VMEM((kv, count * rows, HEAD_SIZE), jnp.bfloat16),
            pltpu.VMEM((kv, count * rows, 2 * HEAD_SIZE), jnp.bfloat16),
        ],
        compiler_params=params,
        cost_estimate=pl.CostEstimate(
            flops=heads * 2 * rows * 2 * count * rows * HEAD_SIZE * 4, bytes_accessed=12_000_000,
            transcendentals=heads * 2 * count * rows * rows,
        ),
        name="far",
    )(q, acc, stat, remote_bias, *arrived)
    return out[None]


def solution(mesh):
    in_specs = (
        P("section", None, ("groups", "ctx"), "head"),
        P("section", None, ("groups", "ctx"), "head"),
        P("section", None, ("groups", "ctx"), "head"),
        P("section", "head", "groups"),
        P("section", "head", "groups"),
    )
    out_specs = P("section", None, ("groups", "ctx"), "head")
    return jax.shard_map(
        per_device, mesh=mesh, in_specs=in_specs, out_specs=out_specs, check_vma=False
    )
```

```python
import functools
import math

import jax
import jax.numpy as jnp
from jax import lax
from jax.experimental import pallas as pl
from jax.experimental.pallas import tpu as pltpu
from jax.sharding import PartitionSpec as P

HEAD_SIZE = 128
TILE_COLUMNS = 128
MAXT = 2
DEAD = -1e30
SCALE2 = math.log2(math.e) / math.sqrt(HEAD_SIZE)
VMEM_BYTES = 24 * 1024 * 1024
REACH = 100.0


def dot_nt(a, b):
    return lax.dot_general(a, b, (((1,), (1,)), ((), ())), preferred_element_type=jnp.float32)


def dot_nn(a, b):
    return lax.dot_general(a, b, (((1,), (0,)), ((), ())), preferred_element_type=jnp.float32)


def prep_kernel(n, rows, kv, rank_ref, cols_smem, cols_ref, k_ref, v_ref, *outs):
    payload_refs = outs[: n - 2]
    band_bias_ref, extra_bias_ref, remote_bias_ref = outs[n - 2 : n + 1]
    outbox_ref, marks_ref, slot_ref, count_ref = outs[n + 1 :]
    rank = rank_ref[0]
    half_len = rows * n
    tiles = cols_ref.shape[1] // TILE_COLUMNS
    per_rank = rows // TILE_COLUMNS

    for g in range(kv):
        for s in range(n):
            count_ref[g, s] = 0
            for slot in range(MAXT):
                slot_ref[g, s * MAXT + slot] = -1
        for t in range(tiles):
            owner = cols_smem[g, t * TILE_COLUMNS] % half_len // rows
            seen = count_ref[g, owner]
            slot_ref[g, owner * MAXT + seen] = t
            count_ref[g, owner] = seen + 1

    for g in range(kv):
        lanes = slice(g * HEAD_SIZE, (g + 1) * HEAD_SIZE)
        for slot in range(MAXT):
            tile = jnp.maximum(slot_ref[g, rank * MAXT + slot], 0)
            start = pl.multiple_of(tile * TILE_COLUMNS, TILE_COLUMNS)
            half = cols_smem[g, start] // half_len
            within = cols_ref[pl.ds(g, 1), pl.ds(start, TILE_COLUMNS)] % rows
            hit = lax.broadcasted_iota(jnp.int32, (rows, TILE_COLUMNS), 0) == within
            pick = jnp.where(hit, 1.0, 0.0).astype(jnp.bfloat16)
            for which, ref in enumerate((k_ref, v_ref)):
                source = ref[pl.ds(half, 1), :, lanes][0]
                got = lax.dot_general(
                    pick, source, (((0,), (0,)), ((), ())), preferred_element_type=jnp.float32
                )
                outbox_ref[which, slot * TILE_COLUMNS : (slot + 1) * TILE_COLUMNS, lanes] = (
                    got.astype(jnp.bfloat16)
                )
    for i, ref in enumerate(payload_refs):
        d = i + 2

        @pl.when(rank + d < n)
        def _():
            ref[...] = outbox_ref[...]

        @pl.when(rank + d >= n)
        def _():
            ref[0] = k_ref[0]
            ref[1] = v_ref[0]

    blocks = 2 * n * per_rank
    dead_row = jnp.full((1, rows), DEAD, jnp.float32)
    for g in range(kv):
        cols = cols_ref[g : g + 1, :]
        high = lax.broadcasted_iota(jnp.int32, (blocks, cols.shape[1]), 0) == cols // TILE_COLUMNS
        low = lax.broadcasted_iota(jnp.int32, (TILE_COLUMNS, cols.shape[1]), 0) == cols % TILE_COLUMNS
        count = dot_nt(
            jnp.where(high, 1.0, 0.0).astype(jnp.bfloat16),
            jnp.where(low, 1.0, 0.0).astype(jnp.bfloat16),
        )
        marks_ref[g] = jnp.where(count > 0.5, 0.0, DEAD)

        def marks_of(half, s):
            first = (half * n + s) * per_rank
            return jnp.concatenate(
                [marks_ref[g, pl.ds(first + i, 1), :] for i in range(per_rank)], axis=1
            )

        first_rank = rank == 0
        before = jnp.where(first_rank, n - 1, rank - 1)
        before_low = marks_of(0, before)
        own_low = marks_of(0, rank)
        own_high = marks_of(1, rank)
        before_high = marks_of(jnp.where(first_rank, 0, 1), before)
        band_bias_ref[g, 0:1, :rows] = jnp.where(first_rank, dead_row, before_low)
        band_bias_ref[g, 0:1, rows:] = own_low
        band_bias_ref[g, 1:2, :rows] = before_high
        band_bias_ref[g, 1:2, rows:] = own_high
        extra_bias_ref[g, 0:1, :rows] = own_low
        extra_bias_ref[g, 0:1, rows:] = jnp.where(first_rank, dead_row, before_low)
        for i in range(n - 2):
            d = i + 2
            earlier = rank >= d
            s = jnp.where(earlier, rank - d, rank - d + n)
            raw = marks_of(0, s)
            for slot in range(MAXT):
                tile = slot_ref[g, s * MAXT + slot]
                half = cols_smem[g, jnp.maximum(tile, 0) * TILE_COLUMNS] // half_len
                live = tile >= 0
                high_value = jnp.where(live, 0.0, DEAD)
                low_value = jnp.where(live & (half == 0) & earlier, 0.0, DEAD)
                span = slice(i * rows + slot * TILE_COLUMNS, i * rows + (slot + 1) * TILE_COLUMNS)
                part = slice(slot * TILE_COLUMNS, (slot + 1) * TILE_COLUMNS)
                remote_bias_ref[g, 0:1, span] = jnp.full((1, TILE_COLUMNS), low_value, jnp.float32)
                remote_bias_ref[g, 1:2, span] = jnp.where(
                    earlier, jnp.full((1, TILE_COLUMNS), high_value, jnp.float32), raw[:, part]
                )


def lane_sums(x):
    ones = jnp.ones((x.shape[1], HEAD_SIZE), jnp.bfloat16)
    return dot_nn(x.astype(jnp.bfloat16), ones)


def folded(x, op):
    while x.shape[0] > 8:
        half = x.shape[0] // 2
        x = op(x[:half], x[half:])
    return x


def norms(x):
    x = x.astype(jnp.float32)
    return lane_sums(x * x)


def in_range(query_norm, key_norm, lowest):
    bound = jnp.sqrt(jnp.max(query_norm)) * jnp.sqrt(jnp.max(key_norm)) * (1.02 * SCALE2)
    return bound - jnp.min(lowest) <= REACH


def lanes_of(head):
    return pl.ds(pl.multiple_of(head * HEAD_SIZE, HEAD_SIZE), HEAD_SIZE)


def split_keys(k_ref, v_ref, kv, rows, keys_ref, values_ref, second=None):
    ones = jnp.ones((2 * rows, HEAD_SIZE), jnp.bfloat16)
    for g in range(kv):
        lanes = slice(g * HEAD_SIZE, (g + 1) * HEAD_SIZE)
        for ref, to in ((k_ref, keys_ref), (v_ref, values_ref)):
            low, high = ref[0, :, lanes], ref[1, :, lanes]
            to[g, :rows, :HEAD_SIZE] = low
            to[g, rows:, :HEAD_SIZE] = high if second is None else jnp.where(second, low, high)
        values_ref[g, :, HEAD_SIZE:] = ones


def slash_blocks(slash_ref, head, t):
    base = jnp.broadcast_to(slash_ref[head], (t, 4 * t))
    rolled = pltpu.roll(base, 1, 1, stride=1, stride_axis=0)
    return rolled[:, :t], rolled[:, t : 2 * t], rolled[:, 2 * t : 3 * t]


def weights_of(blocks, shift):
    return [jnp.exp2(x - shift).astype(jnp.bfloat16) for x in blocks]


def row_max(blocks):
    x = functools.reduce(jnp.maximum, blocks)
    return jnp.broadcast_to(jnp.max(x, axis=1, keepdims=True), x.shape)


def columns_of(s, count):
    return [s[:, b * HEAD_SIZE : (b + 1) * HEAD_SIZE] for b in range(count)]


def own_kernel(
    rows, kv, group_size,
    q_ref, k_ref, v_ref, band_bias_ref, extra_bias_ref, slash_ref,
    acc_ref, sum_ref, shift_ref, gauge_ref, qcopy_ref,
    keys_ref, values_ref, tri_ref,
):
    t = rows // 2
    tri = lax.broadcasted_iota(jnp.int32, (t, t), 0) >= lax.broadcasted_iota(jnp.int32, (t, t), 1)
    split_keys(k_ref, v_ref, kv, rows, keys_ref, values_ref)
    qcopy_ref[...] = q_ref[...]
    for g in range(kv):
        for m in range(2):
            for b in range(2):
                row = band_bias_ref[g, m : m + 1, rows + b * t : rows + (b + 1) * t]
                tri_ref[g, m, b] = jnp.where(tri, row, DEAD)

    gauge_ref[0] = jnp.zeros((8, HEAD_SIZE), jnp.float32)
    gauge_ref[1] = jnp.full((8, HEAD_SIZE), -DEAD, jnp.float32)
    blank = jnp.zeros((t, t), jnp.bfloat16)
    for g in range(kv):

        def one_head(h, carry):
            head = g * group_size + h
            at = lanes_of(head)
            _, t1, t0 = slash_blocks(slash_ref, head, t)
            for m in range(2):
                q = q_ref[m, :, at]
                s = dot_nt(q, keys_ref[g, : (m + 1) * rows]) * SCALE2
                band = s[:, m * rows :]
                row = band_bias_ref[g, m : m + 1, rows : rows + t]
                top = [band[:t, :t] + jnp.maximum(t0, tri_ref[g, m, 0])]
                low = [
                    band[t:, :t] + jnp.maximum(t1, row),
                    band[t:, t:] + jnp.maximum(t0, tri_ref[g, m, 1]),
                ]
                if m == 1:
                    more = columns_of(s[:, :rows] + extra_bias_ref[g, :, :rows], 2)
                    top = [x[:t] for x in more] + top
                    low = [x[t:] for x in more] + low
                top_shift, low_shift = row_max(top), row_max(low)
                p = jnp.concatenate(
                    [
                        jnp.concatenate(weights_of(top, top_shift) + [blank], axis=1),
                        jnp.concatenate(weights_of(low, low_shift), axis=1),
                    ],
                    axis=0,
                )
                o = dot_nn(p, values_ref[g, : (m + 1) * rows])
                shift = jnp.concatenate([top_shift, low_shift], axis=0)
                acc_ref[m, :, at] = o[:, :HEAD_SIZE]
                sum_ref[m, :, at] = o[:, HEAD_SIZE:]
                shift_ref[m, :, at] = shift
                gauge_ref[0] = jnp.maximum(gauge_ref[0], folded(norms(q), jnp.maximum))
                gauge_ref[1] = jnp.minimum(gauge_ref[1], folded(shift, jnp.minimum))
            return carry

        lax.fori_loop(0, group_size, one_head, 0, unroll=True)


def before_kernel(
    rows, kv, group_size,
    rank_ref, q_ref, k_ref, v_ref, band_bias_ref, extra_bias_ref, slash_ref, gauge_ref,
    acc_in, sum_in, shift_in,
    acc_ref, sum_ref, shift_ref,
    keys_ref, values_ref,
):
    first_rank = rank_ref[0] == 0
    shut = jnp.where(first_rank, DEAD, 0.0)
    t = rows // 2
    split_keys(k_ref, v_ref, kv, rows, keys_ref, values_ref, first_rank)
    key_norm = jnp.zeros((8, HEAD_SIZE), jnp.float32)
    for g in range(kv):
        key_norm = jnp.maximum(key_norm, folded(norms(keys_ref[g]), jnp.maximum))
    fast = in_range(gauge_ref[0], key_norm, gauge_ref[1])

    def scores(g, m, head, q):
        t2, t1, _ = slash_blocks(slash_ref, head, t)
        if m == 0:
            t2, t1 = t2 + shut, t1 + shut
        s = dot_nt(q, keys_ref[g, : (m + 1) * rows]) * SCALE2
        band = s[:, m * rows :]
        row = [band_bias_ref[g, m : m + 1, b * t : (b + 1) * t] for b in range(2)]
        blocks = [
            jnp.concatenate(
                [band[:t, :t] + jnp.maximum(t2, row[0]), band[t:, :t] + row[0]], axis=0
            ),
            jnp.concatenate(
                [
                    band[:t, t:] + jnp.maximum(t1, row[1]),
                    band[t:, t:] + jnp.maximum(t2, row[1]),
                ],
                axis=0,
            ),
        ]
        if m == 1:
            blocks = columns_of(s[:, :rows] + extra_bias_ref[g, :, rows:], 2) + blocks
        return blocks

    def merge(g, m, at, blocks, shift, shrink):
        p = jnp.concatenate(weights_of(blocks, shift), axis=1)
        o = dot_nn(p, values_ref[g, : (m + 1) * rows])
        acc, total = acc_in[m, :, at], sum_in[m, :, at]
        if shrink is not None:
            acc, total = acc * shrink, total * shrink
        acc_ref[m, :, at] = acc + o[:, :HEAD_SIZE]
        sum_ref[m, :, at] = total + o[:, HEAD_SIZE:]

    @pl.when(fast)
    def _():
        for g in range(kv):

            def one_head(h, carry):
                head = g * group_size + h
                at = lanes_of(head)
                for m in range(2):
                    shift = shift_in[m, :, at]
                    merge(g, m, at, scores(g, m, head, q_ref[m, :, at]), shift, None)
                    shift_ref[m, :, at] = shift
                return carry

            lax.fori_loop(0, group_size, one_head, 0, unroll=True)

    @pl.when(jnp.logical_not(fast))
    def _():
        for g in range(kv):

            def one_head(h, carry):
                head = g * group_size + h
                at = lanes_of(head)
                for m in range(2):
                    blocks = scores(g, m, head, q_ref[m, :, at])
                    old = shift_in[m, :, at]
                    shift = jnp.maximum(old, row_max(blocks))
                    merge(g, m, at, blocks, shift, jnp.exp2(old - shift))
                    shift_ref[m, :, at] = shift
                return carry

            lax.fori_loop(0, group_size, one_head, 0)


def far_kernel(rows, kv, group_size, count, *refs):
    q_ref, acc_ref, sum_ref, shift_ref, gauge_ref, remote_bias_ref = refs[:6]
    arrived = refs[6 : 6 + count]
    out_ref, kr_ref, vr_ref = refs[6 + count :]
    ones = jnp.ones((rows, HEAD_SIZE), jnp.bfloat16)
    key_norm = jnp.zeros((8, HEAD_SIZE), jnp.float32)
    for g in range(kv):
        lanes = slice(g * HEAD_SIZE, (g + 1) * HEAD_SIZE)
        for i, ref in enumerate(arrived):
            at = slice(i * rows, (i + 1) * rows)
            k = ref[0, :, lanes]
            key_norm = jnp.maximum(key_norm, folded(norms(k), jnp.maximum))
            kr_ref[g, at, :] = k
            vr_ref[g, at, :HEAD_SIZE] = ref[1, :, lanes]
            vr_ref[g, at, HEAD_SIZE:] = ones
    fast = in_range(gauge_ref[0], key_norm, gauge_ref[1])

    def scores(g, m, q):
        s = dot_nt(q, kr_ref[g]) * SCALE2 + remote_bias_ref[g, m : m + 1, :]
        return columns_of(s, count * rows // HEAD_SIZE)

    def finish(g, m, at, blocks, shift, shrink):
        o = dot_nn(jnp.concatenate(weights_of(blocks, shift), axis=1), vr_ref[g])
        acc, total = acc_ref[m, :, at], sum_ref[m, :, at]
        if shrink is not None:
            acc, total = acc * shrink, total * shrink
        out = (acc + o[:, :HEAD_SIZE]) / (total + o[:, HEAD_SIZE:])
        out_ref[m, :, at] = out.astype(jnp.bfloat16)

    @pl.when(fast)
    def _():
        for g in range(kv):

            def one_head(h, carry):
                at = lanes_of(g * group_size + h)
                for m in range(2):
                    finish(g, m, at, scores(g, m, q_ref[m, :, at]), shift_ref[m, :, at], None)
                return carry

            lax.fori_loop(0, group_size, one_head, 0, unroll=True)

    @pl.when(jnp.logical_not(fast))
    def _():
        for g in range(kv):

            def one_head(h, carry):
                at = lanes_of(g * group_size + h)
                for m in range(2):
                    blocks = scores(g, m, q_ref[m, :, at])
                    old = shift_ref[m, :, at]
                    shift = jnp.maximum(old, row_max(blocks))
                    finish(g, m, at, blocks, shift, jnp.exp2(old - shift))
                return carry

            lax.fori_loop(0, group_size, one_head, 0)


def per_device(queries, key_row_table, value_row_table, vertical_cols, slash_offsets):
    n = lax.axis_size("ctx")
    rank = lax.axis_index("ctx").astype(jnp.int32)
    rows = queries.shape[2]
    kv = key_row_table.shape[3] // HEAD_SIZE
    heads = queries.shape[3] // HEAD_SIZE
    group_size = heads // kv
    q, k, v = queries[0], key_row_table[0], value_row_table[0]
    cols = vertical_cols[0]
    count = n - 2
    per_rank = rows // TILE_COLUMNS
    vmem = pl.BlockSpec(memory_space=pltpu.VMEM)
    smem = pl.BlockSpec(memory_space=pltpu.SMEM)
    params = pltpu.CompilerParams(vmem_limit_bytes=VMEM_BYTES)
    unit = jax.ShapeDtypeStruct((2, rows, kv * HEAD_SIZE), jnp.bfloat16)
    rank1 = rank[None]

    def shifted(x, d):
        return lax.ppermute(x, "ctx", [(i, (i + d) % n) for i in range(n)])

    k_before, v_before = shifted(k, 1), shifted(v, 1)

    prepared = pl.pallas_call(
        functools.partial(prep_kernel, n, rows, kv),
        out_shape=[unit] * count
        + [
            jax.ShapeDtypeStruct((kv, 2, 2 * rows), jnp.float32),
            jax.ShapeDtypeStruct((kv, 1, 2 * rows), jnp.float32),
            jax.ShapeDtypeStruct((kv, 2, count * rows), jnp.float32),
        ],
        in_specs=[smem, smem, vmem, vmem, vmem],
        out_specs=[vmem] * (3 + count),
        scratch_shapes=[
            pltpu.VMEM((2, rows, kv * HEAD_SIZE), jnp.bfloat16),
            pltpu.VMEM((kv, 2 * n * per_rank, TILE_COLUMNS), jnp.float32),
            pltpu.SMEM((kv, n * MAXT), jnp.int32),
            pltpu.SMEM((kv, n), jnp.int32),
        ],
        compiler_params=params,
        name="prep",
    )(rank1, cols, cols, k, v)
    band_bias, extra_bias, remote_bias = prepared[count:]
    arrived = [shifted(x, i + 2) for i, x in enumerate(prepared[:count])]

    reach = rows - 1 - jnp.arange(2 * rows, dtype=jnp.int32)
    hit = jnp.any(slash_offsets[0][:, :, None] == reach[None, None, :], axis=1)
    slash = jnp.where(hit, 0.0, DEAD).astype(jnp.float32)[:, None, :]

    state = jax.ShapeDtypeStruct((2, rows, heads * HEAD_SIZE), jnp.float32)
    keys_scratch = pltpu.VMEM((kv, 2 * rows, HEAD_SIZE), jnp.bfloat16)
    values_scratch = pltpu.VMEM((kv, 2 * rows, 2 * HEAD_SIZE), jnp.bfloat16)

    def cost(blocks):
        return pl.CostEstimate(
            flops=heads * blocks * rows * rows * HEAD_SIZE * 4,
            bytes_accessed=16_000_000,
            transcendentals=heads * blocks * rows * rows,
        )

    acc, total, shift, gauge, qv = pl.pallas_call(
        functools.partial(own_kernel, rows, kv, group_size),
        out_shape=[
            state,
            state,
            state,
            jax.ShapeDtypeStruct((2, 8, HEAD_SIZE), jnp.float32),
            jax.ShapeDtypeStruct(q.shape, q.dtype),
        ],
        in_specs=[vmem] * 6,
        out_specs=[vmem] * 5,
        scratch_shapes=[
            keys_scratch,
            values_scratch,
            pltpu.VMEM((kv, 2, 2, rows // 2, rows // 2), jnp.float32),
        ],
        compiler_params=params,
        cost_estimate=cost(3),
        name="own",
    )(q, k, v, band_bias, extra_bias, slash)

    acc, total, shift = pl.pallas_call(
        functools.partial(before_kernel, rows, kv, group_size),
        out_shape=[state] * 3,
        in_specs=[smem] + [vmem] * 10,
        out_specs=[vmem] * 3,
        scratch_shapes=[keys_scratch, values_scratch],
        input_output_aliases={8: 0, 9: 1, 10: 2},
        compiler_params=params,
        cost_estimate=cost(3),
        name="before",
    )(
        rank1, qv, k_before, v_before, band_bias, extra_bias, slash, gauge, acc, total, shift
    )

    out = pl.pallas_call(
        functools.partial(far_kernel, rows, kv, group_size, count),
        out_shape=jax.ShapeDtypeStruct(q.shape, jnp.bfloat16),
        in_specs=[vmem] * (6 + count),
        out_specs=vmem,
        scratch_shapes=[
            pltpu.VMEM((kv, count * rows, HEAD_SIZE), jnp.bfloat16),
            pltpu.VMEM((kv, count * rows, 2 * HEAD_SIZE), jnp.bfloat16),
        ],
        compiler_params=params,
        cost_estimate=cost(2 * count),
        name="far",
    )(qv, acc, total, shift, gauge, remote_bias, *arrived)
    return out[None]


def solution(mesh):
    in_specs = (
        P("section", None, ("groups", "ctx"), "head"),
        P("section", None, ("groups", "ctx"), "head"),
        P("section", None, ("groups", "ctx"), "head"),
        P("section", "head", "groups"),
        P("section", "head", "groups"),
    )
    out_specs = P("section", None, ("groups", "ctx"), "head")
    return jax.shard_map(
        per_device, mesh=mesh, in_specs=in_specs, out_specs=out_specs, check_vma=False
    )
```

```python
import functools
import math

import jax
import jax.numpy as jnp
from jax import lax
from jax.experimental import pallas as pl
from jax.experimental.pallas import tpu as pltpu
from jax.sharding import PartitionSpec as P

HEAD_SIZE = 128
TILE_COLUMNS = 128
MAXT = 2
DEAD = -1e30
SCALE2 = math.log2(math.e) / math.sqrt(HEAD_SIZE)
VMEM_BYTES = 24 * 1024 * 1024
REACH = 100.0


def dot_nt(a, b):
    return lax.dot_general(a, b, (((1,), (1,)), ((), ())), preferred_element_type=jnp.float32)


def dot_nn(a, b):
    return lax.dot_general(a, b, (((1,), (0,)), ((), ())), preferred_element_type=jnp.float32)


def prep_kernel(n, rows, kv, rank_ref, cols_smem, cols_ref, k_ref, v_ref, *outs):
    parts = (n - 3) * kv
    split_refs, whole_ref = outs[:parts], outs[parts]
    band_bias_ref, extra_bias_ref, remote_bias_ref, kcopy_ref, vcopy_ref = outs[parts + 1 : parts + 6]
    outbox_ref, marks_ref, slot_ref, count_ref = outs[parts + 6 :]
    kcopy_ref[...] = k_ref[...]
    vcopy_ref[...] = v_ref[...]
    rank = rank_ref[0]
    half_len = rows * n
    tiles = cols_ref.shape[1] // TILE_COLUMNS
    per_rank = rows // TILE_COLUMNS

    for g in range(kv):
        for s in range(n):
            count_ref[g, s] = 0
            for slot in range(MAXT):
                slot_ref[g, s * MAXT + slot] = -1
        for t in range(tiles):
            owner = cols_smem[g, t * TILE_COLUMNS] % half_len // rows
            seen = count_ref[g, owner]
            slot_ref[g, owner * MAXT + seen] = t
            count_ref[g, owner] = seen + 1

    for g in range(kv):
        lanes = slice(g * HEAD_SIZE, (g + 1) * HEAD_SIZE)
        for slot in range(MAXT):
            tile = jnp.maximum(slot_ref[g, rank * MAXT + slot], 0)
            start = pl.multiple_of(tile * TILE_COLUMNS, TILE_COLUMNS)
            half = cols_smem[g, start] // half_len
            within = cols_ref[pl.ds(g, 1), pl.ds(start, TILE_COLUMNS)] % rows
            hit = lax.broadcasted_iota(jnp.int32, (rows, TILE_COLUMNS), 0) == within
            pick = jnp.where(hit, 1.0, 0.0).astype(jnp.bfloat16)
            for which, ref in enumerate((k_ref, v_ref)):
                source = ref[pl.ds(half, 1), :, lanes][0]
                got = lax.dot_general(
                    pick, source, (((0,), (0,)), ((), ())), preferred_element_type=jnp.float32
                )
                outbox_ref[which, slot * TILE_COLUMNS : (slot + 1) * TILE_COLUMNS, lanes] = (
                    got.astype(jnp.bfloat16)
                )
    for i in range(n - 2):
        later = rank + i + 2 < n
        refs = [whole_ref] if i == n - 3 else split_refs[i * kv : (i + 1) * kv]
        wide = kv * HEAD_SIZE // len(refs)

        @pl.when(later)
        def _():
            for j, ref in enumerate(refs):
                ref[...] = outbox_ref[:, :, j * wide : (j + 1) * wide]

        @pl.when(jnp.logical_not(later))
        def _():
            for j, ref in enumerate(refs):
                ref[0] = k_ref[0, :, j * wide : (j + 1) * wide]
                ref[1] = v_ref[0, :, j * wide : (j + 1) * wide]

    blocks = 2 * n * per_rank
    dead_row = jnp.full((1, rows), DEAD, jnp.float32)
    for g in range(kv):
        cols = cols_ref[g : g + 1, :]
        high = lax.broadcasted_iota(jnp.int32, (blocks, cols.shape[1]), 0) == cols // TILE_COLUMNS
        low = lax.broadcasted_iota(jnp.int32, (TILE_COLUMNS, cols.shape[1]), 0) == cols % TILE_COLUMNS
        count = dot_nt(
            jnp.where(high, 1.0, 0.0).astype(jnp.bfloat16),
            jnp.where(low, 1.0, 0.0).astype(jnp.bfloat16),
        )
        marks_ref[g] = jnp.where(count > 0.5, 0.0, DEAD)

        def marks_of(half, s):
            first = (half * n + s) * per_rank
            return jnp.concatenate(
                [marks_ref[g, pl.ds(first + i, 1), :] for i in range(per_rank)], axis=1
            )

        first_rank = rank == 0
        before = jnp.where(first_rank, n - 1, rank - 1)
        before_low = marks_of(0, before)
        own_low = marks_of(0, rank)
        own_high = marks_of(1, rank)
        before_high = marks_of(jnp.where(first_rank, 0, 1), before)
        band_bias_ref[g, 0:1, :rows] = jnp.where(first_rank, dead_row, before_low)
        band_bias_ref[g, 0:1, rows:] = own_low
        band_bias_ref[g, 1:2, :rows] = before_high
        band_bias_ref[g, 1:2, rows:] = own_high
        extra_bias_ref[g, 0:1, :rows] = own_low
        extra_bias_ref[g, 0:1, rows:] = jnp.where(first_rank, dead_row, before_low)
        for i in range(n - 2):
            d = i + 2
            earlier = rank >= d
            s = jnp.where(earlier, rank - d, rank - d + n)
            raw = marks_of(0, s)
            for slot in range(MAXT):
                tile = slot_ref[g, s * MAXT + slot]
                half = cols_smem[g, jnp.maximum(tile, 0) * TILE_COLUMNS] // half_len
                live = tile >= 0
                high_value = jnp.where(live, 0.0, DEAD)
                low_value = jnp.where(live & (half == 0) & earlier, 0.0, DEAD)
                span = slice(i * rows + slot * TILE_COLUMNS, i * rows + (slot + 1) * TILE_COLUMNS)
                part = slice(slot * TILE_COLUMNS, (slot + 1) * TILE_COLUMNS)
                remote_bias_ref[g, 0:1, span] = jnp.full((1, TILE_COLUMNS), low_value, jnp.float32)
                remote_bias_ref[g, 1:2, span] = jnp.where(
                    earlier, jnp.full((1, TILE_COLUMNS), high_value, jnp.float32), raw[:, part]
                )


def lane_sums(x):
    ones = jnp.ones((x.shape[1], HEAD_SIZE), jnp.bfloat16)
    return dot_nn(x.astype(jnp.bfloat16), ones)


def folded(x, op):
    while x.shape[0] > 8:
        half = x.shape[0] // 2
        x = op(x[:half], x[half:])
    return x


def norms(x):
    x = x.astype(jnp.float32)
    return lane_sums(x * x)


def in_range(query_norm, key_norm, lowest):
    bound = jnp.sqrt(jnp.max(query_norm)) * jnp.sqrt(jnp.max(key_norm)) * (1.02 * SCALE2)
    return bound - jnp.min(lowest) <= REACH


def lanes_of(head):
    return pl.ds(pl.multiple_of(head * HEAD_SIZE, HEAD_SIZE), HEAD_SIZE)


def split_keys(k_ref, v_ref, kv, rows, keys_ref, values_ref):
    ones = jnp.ones((2 * rows, HEAD_SIZE), jnp.bfloat16)
    for g in range(kv):
        lanes = slice(g * HEAD_SIZE, (g + 1) * HEAD_SIZE)
        for ref, to in ((k_ref, keys_ref), (v_ref, values_ref)):
            to[g, :rows, :HEAD_SIZE] = ref[0, :, lanes]
            to[g, rows:, :HEAD_SIZE] = ref[1, :, lanes]
        values_ref[g, :, HEAD_SIZE:] = ones


def slash_blocks(slash_ref, head, t):
    base = jnp.broadcast_to(slash_ref[head], (t, 4 * t))
    rolled = pltpu.roll(base, 1, 1, stride=1, stride_axis=0)
    return rolled[:, :t], rolled[:, t : 2 * t], rolled[:, 2 * t : 3 * t]


def weights_of(blocks, shift):
    return [jnp.exp2(x - shift).astype(jnp.bfloat16) for x in blocks]


def row_max(blocks):
    x = functools.reduce(jnp.maximum, blocks)
    return jnp.broadcast_to(jnp.max(x, axis=1, keepdims=True), x.shape)


def columns_of(s, count):
    return [s[:, b * HEAD_SIZE : (b + 1) * HEAD_SIZE] for b in range(count)]


def make_slash(offsets_ref, slash_ref, rows, heads):
    count = offsets_ref.shape[2]
    reach = rows - 1 - lax.broadcasted_iota(jnp.int32, (rows, count), 0)
    ones = jnp.ones((8, count), jnp.bfloat16)
    for head in range(heads):
        hit = jnp.where(reach == offsets_ref[head], 1.0, 0.0).astype(jnp.bfloat16)
        found = dot_nt(ones, hit)[:1]
        slash_ref[head, :, :rows] = jnp.where(found > 0.5, 0.0, DEAD)
        slash_ref[head, :, rows:] = jnp.full((1, rows), DEAD, jnp.float32)


def hold_kernel(rows, heads, late, offsets_ref, q_ref, *refs):
    slash_ref, qcopy_ref = refs[late : late + 2]
    make_slash(offsets_ref, slash_ref, rows, heads)
    qcopy_ref[...] = q_ref[...]
    for a, b in zip(refs[:late], refs[late + 2 :]):
        b[...] = a[...]


def own_kernel(
    rows, kv, group_size,
    q_ref, k_ref, v_ref, band_bias_ref, extra_bias_ref, slash_ref, *refs,
):
    passed = (len(refs) - 8) // 2
    for a, b in zip(refs[:passed], refs[passed + 5 :]):
        b[...] = a[...]
    acc_ref, sum_ref, shift_ref, gauge_ref, table_ref = refs[passed : passed + 5]
    keys_ref, values_ref, tri_ref = refs[-3:]
    t = rows // 2
    tri = lax.broadcasted_iota(jnp.int32, (t, t), 0) >= lax.broadcasted_iota(jnp.int32, (t, t), 1)
    split_keys(k_ref, v_ref, kv, rows, keys_ref, values_ref)
    for g in range(kv):
        for m in range(2):
            for b in range(2):
                row = band_bias_ref[g, m : m + 1, rows + b * t : rows + (b + 1) * t]
                tri_ref[g, m, b] = jnp.where(tri, row, DEAD)

    gauge_ref[0] = jnp.zeros((8, HEAD_SIZE), jnp.float32)
    gauge_ref[1] = jnp.full((8, HEAD_SIZE), -DEAD, jnp.float32)
    blank = jnp.zeros((t, t), jnp.bfloat16)
    for g in range(kv):

        def one_head(h, carry):
            head = g * group_size + h
            at = lanes_of(head)
            t2, t1, t0 = slash_blocks(slash_ref, head, t)
            table_ref[head, :, :t] = t2
            table_ref[head, :, t:] = t1
            for m in range(2):
                q = q_ref[m, :, at]
                s = dot_nt(q, keys_ref[g, : (m + 1) * rows]) * SCALE2
                band = s[:, m * rows :]
                row = band_bias_ref[g, m : m + 1, rows : rows + t]
                top = [band[:t, :t] + jnp.maximum(t0, tri_ref[g, m, 0])]
                low = [
                    band[t:, :t] + jnp.maximum(t1, row),
                    band[t:, t:] + jnp.maximum(t0, tri_ref[g, m, 1]),
                ]
                if m == 1:
                    more = columns_of(s[:, :rows] + extra_bias_ref[g, :, :rows], 2)
                    top = [x[:t] for x in more] + top
                    low = [x[t:] for x in more] + low
                top_shift, low_shift = row_max(top), row_max(low)
                p = jnp.concatenate(
                    [
                        jnp.concatenate(weights_of(top, top_shift) + [blank], axis=1),
                        jnp.concatenate(weights_of(low, low_shift), axis=1),
                    ],
                    axis=0,
                )
                o = dot_nn(p, values_ref[g, : (m + 1) * rows])
                shift = jnp.concatenate([top_shift, low_shift], axis=0)
                acc_ref[m, :, at] = o[:, :HEAD_SIZE]
                sum_ref[m, :, at] = o[:, HEAD_SIZE:]
                shift_ref[m, :, at] = shift
                gauge_ref[0] = jnp.maximum(gauge_ref[0], folded(norms(q), jnp.maximum))
                gauge_ref[1] = jnp.minimum(gauge_ref[1], folded(shift, jnp.minimum))
            return carry

        lax.fori_loop(0, group_size, one_head, 0, unroll=True)


def middle_kernel(
    rows, kv, group_size,
    rank_ref, q_ref, k_ref, v_ref, first_ref, band_bias_ref, extra_bias_ref, remote_bias_ref,
    table_ref, gauge_ref, acc_in, sum_in, shift_in,
    acc_ref, sum_ref, shift_ref,
    keys_ref, values_ref,
):
    first_rank = rank_ref[0] == 0
    shut = jnp.where(first_rank, DEAD, 0.0)
    t = rows // 2
    ones = jnp.ones((3 * rows, HEAD_SIZE), jnp.bfloat16)
    key_norm = jnp.zeros((8, HEAD_SIZE), jnp.float32)
    for g in range(kv):
        lanes = slice(g * HEAD_SIZE, (g + 1) * HEAD_SIZE)
        for which, ref, to in ((0, k_ref, keys_ref), (1, v_ref, values_ref)):
            low, high = ref[0, :, lanes], ref[1, :, lanes]
            to[g, :rows, :HEAD_SIZE] = jnp.where(first_rank, low, high)
            to[g, rows : 2 * rows, :HEAD_SIZE] = low
            to[g, 2 * rows :, :HEAD_SIZE] = first_ref[which, :, lanes]
        values_ref[g, :, HEAD_SIZE:] = ones
        for part in range(3):
            k = keys_ref[g, part * rows : (part + 1) * rows]
            key_norm = jnp.maximum(key_norm, folded(norms(k), jnp.maximum))
    fast = in_range(gauge_ref[0], key_norm, gauge_ref[1])

    def scores(g, m, head, q):
        t2, t1 = table_ref[head, :, :t], table_ref[head, :, t:]
        if m == 0:
            t2, t1 = t2 + shut, t1 + shut
        s = dot_nt(q, keys_ref[g, (1 - m) * rows :]) * SCALE2
        band = s[:, :rows]
        row = [band_bias_ref[g, m : m + 1, b * t : (b + 1) * t] for b in range(2)]
        blocks = [
            jnp.concatenate(
                [band[:t, :t] + jnp.maximum(t2, row[0]), band[t:, :t] + row[0]], axis=0
            ),
            jnp.concatenate(
                [
                    band[:t, t:] + jnp.maximum(t1, row[1]),
                    band[t:, t:] + jnp.maximum(t2, row[1]),
                ],
                axis=0,
            ),
        ]
        if m == 1:
            blocks += columns_of(s[:, rows : 2 * rows] + extra_bias_ref[g, :, rows:], 2)
        return blocks + columns_of(s[:, (m + 1) * rows :] + remote_bias_ref[g, m : m + 1, -rows:], 2)

    def merge(g, m, at, blocks, shift, shrink):
        p = jnp.concatenate(weights_of(blocks, shift), axis=1)
        o = dot_nn(p, values_ref[g, (1 - m) * rows :])
        acc, total = acc_in[m, :, at], sum_in[m, :, at]
        if shrink is not None:
            acc, total = acc * shrink, total * shrink
        acc_ref[m, :, at] = acc + o[:, :HEAD_SIZE]
        sum_ref[m, :, at] = total + o[:, HEAD_SIZE:]

    @pl.when(fast)
    def _():
        for g in range(kv):

            def one_head(h, carry):
                head = g * group_size + h
                at = lanes_of(head)
                for m in range(2):
                    shift = shift_in[m, :, at]
                    merge(g, m, at, scores(g, m, head, q_ref[m, :, at]), shift, None)
                    shift_ref[m, :, at] = shift
                return carry

            lax.fori_loop(0, group_size, one_head, 0, unroll=True)

    @pl.when(jnp.logical_not(fast))
    def _():
        for g in range(kv):

            def one_head(h, carry):
                head = g * group_size + h
                at = lanes_of(head)
                for m in range(2):
                    blocks = scores(g, m, head, q_ref[m, :, at])
                    old = shift_in[m, :, at]
                    shift = jnp.maximum(old, row_max(blocks))
                    merge(g, m, at, blocks, shift, jnp.exp2(old - shift))
                    shift_ref[m, :, at] = shift
                return carry

            lax.fori_loop(0, group_size, one_head, 0)


def far_kernel(rows, g, group_size, count, *refs):
    q_ref, acc_ref, sum_ref, shift_ref, gauge_ref, remote_bias_ref = refs[:6]
    arrived = refs[6 : 6 + count]
    out_hbm, keys_ref, values_ref, out_ref, sems = refs[-5:]
    ones = jnp.ones((rows, HEAD_SIZE), jnp.bfloat16)
    key_norm = jnp.zeros((8, HEAD_SIZE), jnp.float32)
    for i, ref in enumerate(arrived):
        at = slice(i * rows, (i + 1) * rows)
        k = ref[0]
        key_norm = jnp.maximum(key_norm, folded(norms(k), jnp.maximum))
        keys_ref[at, :] = k
        values_ref[at, :HEAD_SIZE] = ref[1]
        values_ref[at, HEAD_SIZE:] = ones
    fast = in_range(gauge_ref[0], key_norm, gauge_ref[1])
    copies = [
        pltpu.make_async_copy(
            out_ref.at[h], out_hbm.at[:, :, lanes_of(g * group_size + h)], sems.at[h]
        )
        for h in range(group_size)
    ]

    def scores(m, q):
        bias = remote_bias_ref[g, m : m + 1, : count * rows]
        s = dot_nt(q, keys_ref[...]) * SCALE2 + bias
        return columns_of(s, count * rows // HEAD_SIZE)

    def finish(h, m, at, blocks, shift, shrink):
        o = dot_nn(jnp.concatenate(weights_of(blocks, shift), axis=1), values_ref[...])
        acc, total = acc_ref[m, :, at], sum_ref[m, :, at]
        if shrink is not None:
            acc, total = acc * shrink, total * shrink
        out = (acc + o[:, :HEAD_SIZE]) / (total + o[:, HEAD_SIZE:])
        out_ref[h, m] = out.astype(jnp.bfloat16)

    for h in range(group_size):
        at = lanes_of(g * group_size + h)
        for m in range(2):
            finish(h, m, at, scores(m, q_ref[m, :, at]), shift_ref[m, :, at], None)
        copies[h].start()
    for copy in copies:
        copy.wait()

    @pl.when(jnp.logical_not(fast))
    def _():
        def one_head(h, carry):
            at = lanes_of(g * group_size + h)
            for m in range(2):
                blocks = scores(m, q_ref[m, :, at])
                old = shift_ref[m, :, at]
                shift = jnp.maximum(old, row_max(blocks))
                finish(h, m, at, blocks, shift, jnp.exp2(old - shift))
            return carry

        lax.fori_loop(0, group_size, one_head, 0)
        for copy in copies:
            copy.start()
        for copy in copies:
            copy.wait()


def per_device(queries, key_row_table, value_row_table, vertical_cols, slash_offsets):
    n = lax.axis_size("ctx")
    rank = lax.axis_index("ctx").astype(jnp.int32)
    rows = queries.shape[2]
    kv = key_row_table.shape[3] // HEAD_SIZE
    heads = queries.shape[3] // HEAD_SIZE
    group_size = heads // kv
    q, k, v = queries[0], key_row_table[0], value_row_table[0]
    cols = vertical_cols[0]
    offsets = jnp.swapaxes(slash_offsets, 0, 1)
    count = n - 2
    late = n - 3
    per_rank = rows // TILE_COLUMNS
    vmem = pl.BlockSpec(memory_space=pltpu.VMEM)
    smem = pl.BlockSpec(memory_space=pltpu.SMEM)
    hbm = pl.BlockSpec(memory_space=pl.ANY)
    params = pltpu.CompilerParams(vmem_limit_bytes=VMEM_BYTES)
    unit = jax.ShapeDtypeStruct((2, rows, kv * HEAD_SIZE), jnp.bfloat16)
    piece = jax.ShapeDtypeStruct((2, rows, HEAD_SIZE), jnp.bfloat16)
    rank1 = rank[None]

    def shifted(x, d):
        return lax.ppermute(x, "ctx", [(i, (i + d) % n) for i in range(n)])

    k_before, v_before = shifted(k, 1), shifted(v, 1)

    prepared = pl.pallas_call(
        functools.partial(prep_kernel, n, rows, kv),
        out_shape=[piece] * (late * kv)
        + [unit]
        + [
            jax.ShapeDtypeStruct((kv, 2, 2 * rows), jnp.float32),
            jax.ShapeDtypeStruct((kv, 1, 2 * rows), jnp.float32),
            jax.ShapeDtypeStruct((kv, 2, count * rows), jnp.float32),
            jax.ShapeDtypeStruct(k.shape, k.dtype),
            jax.ShapeDtypeStruct(v.shape, v.dtype),
        ],
        in_specs=[smem, smem, vmem, vmem, vmem],
        out_specs=[vmem] * (6 + late * kv),
        scratch_shapes=[
            pltpu.VMEM((2, rows, kv * HEAD_SIZE), jnp.bfloat16),
            pltpu.VMEM((kv, 2 * n * per_rank, TILE_COLUMNS), jnp.float32),
            pltpu.SMEM((kv, n * MAXT), jnp.int32),
            pltpu.SMEM((kv, n), jnp.int32),
        ],
        compiler_params=params,
        name="prep",
    )(rank1, cols, cols, k, v)
    pieces = prepared[: late * kv]
    whole, band_bias, extra_bias, remote_bias, kv_k, kv_v = prepared[late * kv :]
    first = shifted(whole, n - 1)

    state = jax.ShapeDtypeStruct((2, rows, heads * HEAD_SIZE), jnp.float32)
    keys_scratch = pltpu.VMEM((kv, 2 * rows, HEAD_SIZE), jnp.bfloat16)
    values_scratch = pltpu.VMEM((kv, 2 * rows, 2 * HEAD_SIZE), jnp.bfloat16)

    def cost(blocks):
        return pl.CostEstimate(
            flops=heads * blocks * rows * rows * HEAD_SIZE * 4,
            bytes_accessed=16_000_000,
            transcendentals=heads * blocks * rows * rows,
        )

    slash, qv, *held = pl.pallas_call(
        functools.partial(hold_kernel, rows, heads, late),
        out_shape=[
            jax.ShapeDtypeStruct((heads, 1, 2 * rows), jnp.float32),
            jax.ShapeDtypeStruct(q.shape, q.dtype),
        ]
        + [piece] * late,
        in_specs=[vmem] * (2 + late),
        out_specs=[vmem] * (2 + late),
        compiler_params=params,
        name="hold",
    )(offsets, q, *pieces[::kv])
    arrived = [[shifted(x, i + 2) for i, x in enumerate(held)]]

    rest = [x for i, x in enumerate(pieces) if i % kv]
    acc, total, shift, gauge, table, *rest = pl.pallas_call(
        functools.partial(own_kernel, rows, kv, group_size),
        out_shape=[
            state,
            state,
            state,
            jax.ShapeDtypeStruct((2, 8, HEAD_SIZE), jnp.float32),
            jax.ShapeDtypeStruct((heads, rows // 2, rows), jnp.float32),
        ]
        + [piece] * len(rest),
        in_specs=[vmem] * (6 + len(rest)),
        out_specs=[vmem] * (5 + len(rest)),
        scratch_shapes=[
            keys_scratch,
            values_scratch,
            pltpu.VMEM((kv, 2, 2, rows // 2, rows // 2), jnp.float32),
        ],
        compiler_params=params,
        cost_estimate=cost(3),
        name="own",
    )(qv, kv_k, kv_v, band_bias, extra_bias, slash, *rest)
    for g in range(kv - 1):
        arrived.append([shifted(x, i + 2) for i, x in enumerate(rest[g :: kv - 1])])

    acc, total, shift = pl.pallas_call(
        functools.partial(middle_kernel, rows, kv, group_size),
        out_shape=[state] * 3,
        in_specs=[smem] + [vmem] * 12,
        out_specs=[vmem] * 3,
        scratch_shapes=[
            pltpu.VMEM((kv, 3 * rows, HEAD_SIZE), jnp.bfloat16),
            pltpu.VMEM((kv, 3 * rows, 2 * HEAD_SIZE), jnp.bfloat16),
        ],
        input_output_aliases={10: 0, 11: 1, 12: 2},
        compiler_params=params,
        cost_estimate=cost(5),
        name="middle",
    )(
        rank1, qv, k_before, v_before, first, band_bias, extra_bias, remote_bias, table, gauge,
        acc, total, shift,
    )

    out = []
    for g in range(kv):
        out = [
            pl.pallas_call(
                functools.partial(far_kernel, rows, g, group_size, late),
                out_shape=jax.ShapeDtypeStruct(q.shape, jnp.bfloat16),
                in_specs=[vmem] * (6 + late) + [hbm] * len(out),
                out_specs=hbm,
                scratch_shapes=[
                    pltpu.VMEM((late * rows, HEAD_SIZE), jnp.bfloat16),
                    pltpu.VMEM((late * rows, 2 * HEAD_SIZE), jnp.bfloat16),
                    pltpu.VMEM((group_size, 2, rows, HEAD_SIZE), jnp.bfloat16),
                    pltpu.SemaphoreType.DMA((group_size,)),
                ],
                input_output_aliases={6 + late: 0} if out else {},
                compiler_params=params,
                cost_estimate=cost(late),
                name="far",
            )(qv, acc, total, shift, gauge, remote_bias, *arrived[g], *out)
        ]
    return out[0][None]


def solution(mesh):
    in_specs = (
        P("section", None, ("groups", "ctx"), "head"),
        P("section", None, ("groups", "ctx"), "head"),
        P("section", None, ("groups", "ctx"), "head"),
        P("section", "head", "groups"),
        P("section", "head", "groups"),
    )
    out_specs = P("section", None, ("groups", "ctx"), "head")
    return jax.shard_map(
        per_device, mesh=mesh, in_specs=in_specs, out_specs=out_specs, check_vma=False
    )
```

```python
import functools
import math

import jax
import jax.numpy as jnp
from jax import lax
from jax.experimental import pallas as pl
from jax.experimental.pallas import tpu as pltpu
from jax.sharding import PartitionSpec as P

HEAD_SIZE = 128
TILE_COLUMNS = 128
MAXT = 2
DEAD = -1e30
SCALE2 = math.log2(math.e) / math.sqrt(HEAD_SIZE)
VMEM_BYTES = 24 * 1024 * 1024
REACH = 100.0


def dot_nt(a, b):
    return lax.dot_general(a, b, (((1,), (1,)), ((), ())), preferred_element_type=jnp.float32)


def dot_nn(a, b):
    return lax.dot_general(a, b, (((1,), (0,)), ((), ())), preferred_element_type=jnp.float32)


def prep_kernel(n, rows, kv, rank_ref, cols_smem, cols_ref, k_ref, v_ref, *outs):
    parts = (n - 3) * kv
    split_refs, whole_ref = outs[:parts], outs[parts]
    band_bias_ref, extra_bias_ref, remote_bias_ref, kcopy_ref, vcopy_ref = outs[parts + 1 : parts + 6]
    outbox_ref, marks_ref, slot_ref, count_ref = outs[parts + 6 :]
    kcopy_ref[...] = k_ref[...]
    vcopy_ref[...] = v_ref[...]
    rank = rank_ref[0]
    half_len = rows * n
    tiles = cols_ref.shape[1] // TILE_COLUMNS
    per_rank = rows // TILE_COLUMNS

    for g in range(kv):
        for s in range(n):
            count_ref[g, s] = 0
            for slot in range(MAXT):
                slot_ref[g, s * MAXT + slot] = -1
        for t in range(tiles):
            owner = cols_smem[g, t * TILE_COLUMNS] % half_len // rows
            seen = count_ref[g, owner]
            slot_ref[g, owner * MAXT + seen] = t
            count_ref[g, owner] = seen + 1

    for g in range(kv):
        lanes = slice(g * HEAD_SIZE, (g + 1) * HEAD_SIZE)
        for slot in range(MAXT):
            tile = jnp.maximum(slot_ref[g, rank * MAXT + slot], 0)
            start = pl.multiple_of(tile * TILE_COLUMNS, TILE_COLUMNS)
            half = cols_smem[g, start] // half_len
            within = cols_ref[pl.ds(g, 1), pl.ds(start, TILE_COLUMNS)] % rows
            hit = lax.broadcasted_iota(jnp.int32, (rows, TILE_COLUMNS), 0) == within
            pick = jnp.where(hit, 1.0, 0.0).astype(jnp.bfloat16)
            for which, ref in enumerate((k_ref, v_ref)):
                source = ref[pl.ds(half, 1), :, lanes][0]
                got = lax.dot_general(
                    pick, source, (((0,), (0,)), ((), ())), preferred_element_type=jnp.float32
                )
                outbox_ref[which, slot * TILE_COLUMNS : (slot + 1) * TILE_COLUMNS, lanes] = (
                    got.astype(jnp.bfloat16)
                )
    for i in range(n - 2):
        later = rank + i + 2 < n
        refs = [whole_ref] if i == n - 3 else split_refs[i * kv : (i + 1) * kv]
        wide = kv * HEAD_SIZE // len(refs)

        @pl.when(later)
        def _():
            for j, ref in enumerate(refs):
                ref[...] = outbox_ref[:, :, j * wide : (j + 1) * wide]

        @pl.when(jnp.logical_not(later))
        def _():
            for j, ref in enumerate(refs):
                ref[0] = k_ref[0, :, j * wide : (j + 1) * wide]
                ref[1] = v_ref[0, :, j * wide : (j + 1) * wide]

    blocks = 2 * n * per_rank
    dead_row = jnp.full((1, rows), DEAD, jnp.float32)
    for g in range(kv):
        cols = cols_ref[g : g + 1, :]
        high = lax.broadcasted_iota(jnp.int32, (blocks, cols.shape[1]), 0) == cols // TILE_COLUMNS
        low = lax.broadcasted_iota(jnp.int32, (TILE_COLUMNS, cols.shape[1]), 0) == cols % TILE_COLUMNS
        count = dot_nt(
            jnp.where(high, 1.0, 0.0).astype(jnp.bfloat16),
            jnp.where(low, 1.0, 0.0).astype(jnp.bfloat16),
        )
        marks_ref[g] = jnp.where(count > 0.5, 0.0, DEAD)

        def marks_of(half, s):
            first = (half * n + s) * per_rank
            return jnp.concatenate(
                [marks_ref[g, pl.ds(first + i, 1), :] for i in range(per_rank)], axis=1
            )

        first_rank = rank == 0
        before = jnp.where(first_rank, n - 1, rank - 1)
        before_low = marks_of(0, before)
        own_low = marks_of(0, rank)
        own_high = marks_of(1, rank)
        before_high = marks_of(jnp.where(first_rank, 0, 1), before)
        band_bias_ref[g, 0:1, :rows] = jnp.where(first_rank, dead_row, before_low)
        band_bias_ref[g, 0:1, rows:] = own_low
        band_bias_ref[g, 1:2, :rows] = before_high
        band_bias_ref[g, 1:2, rows:] = own_high
        extra_bias_ref[g, 0:1, :rows] = own_low
        extra_bias_ref[g, 0:1, rows:] = jnp.where(first_rank, dead_row, before_low)
        for i in range(n - 2):
            d = i + 2
            earlier = rank >= d
            s = jnp.where(earlier, rank - d, rank - d + n)
            raw = marks_of(0, s)
            for slot in range(MAXT):
                tile = slot_ref[g, s * MAXT + slot]
                half = cols_smem[g, jnp.maximum(tile, 0) * TILE_COLUMNS] // half_len
                live = tile >= 0
                high_value = jnp.where(live, 0.0, DEAD)
                low_value = jnp.where(live & (half == 0) & earlier, 0.0, DEAD)
                span = slice(i * rows + slot * TILE_COLUMNS, i * rows + (slot + 1) * TILE_COLUMNS)
                part = slice(slot * TILE_COLUMNS, (slot + 1) * TILE_COLUMNS)
                remote_bias_ref[g, 0:1, span] = jnp.full((1, TILE_COLUMNS), low_value, jnp.float32)
                remote_bias_ref[g, 1:2, span] = jnp.where(
                    earlier, jnp.full((1, TILE_COLUMNS), high_value, jnp.float32), raw[:, part]
                )


def lane_sums(x):
    ones = jnp.ones((x.shape[1], HEAD_SIZE), jnp.bfloat16)
    return dot_nn(x.astype(jnp.bfloat16), ones)


def folded(x, op):
    while x.shape[0] > 8:
        half = x.shape[0] // 2
        x = op(x[:half], x[half:])
    return x


def norms(x):
    x = x.astype(jnp.float32)
    return lane_sums(x * x)


def in_range(query_norm, key_norm, lowest):
    bound = jnp.sqrt(jnp.max(query_norm)) * jnp.sqrt(jnp.max(key_norm)) * (1.02 * SCALE2)
    return bound - jnp.min(lowest) <= REACH


def lanes_of(head):
    return pl.ds(pl.multiple_of(head * HEAD_SIZE, HEAD_SIZE), HEAD_SIZE)


def split_keys(k_ref, v_ref, g, rows, keys_ref, values_ref):
    lanes = slice(g * HEAD_SIZE, (g + 1) * HEAD_SIZE)
    for ref, to in ((k_ref, keys_ref), (v_ref, values_ref)):
        to[:rows, :HEAD_SIZE] = ref[0, :, lanes]
        to[rows:, :HEAD_SIZE] = ref[1, :, lanes]
    values_ref[:, HEAD_SIZE:] = jnp.ones((2 * rows, HEAD_SIZE), jnp.bfloat16)


def slash_blocks(slash_ref, head, t):
    base = jnp.broadcast_to(slash_ref[head], (t, 4 * t))
    rolled = pltpu.roll(base, 1, 1, stride=1, stride_axis=0)
    return rolled[:, :t], rolled[:, t : 2 * t], rolled[:, 2 * t : 3 * t]


def weights_of(blocks, shift):
    return [jnp.exp2(x - shift).astype(jnp.bfloat16) for x in blocks]


def row_max(blocks):
    x = functools.reduce(jnp.maximum, blocks)
    return jnp.broadcast_to(jnp.max(x, axis=1, keepdims=True), x.shape)


def columns_of(s, count):
    return [s[:, b * HEAD_SIZE : (b + 1) * HEAD_SIZE] for b in range(count)]


def make_slash(offsets_ref, slash_ref, rows, heads):
    count = offsets_ref.shape[2]
    reach = rows - 1 - lax.broadcasted_iota(jnp.int32, (rows, count), 0)
    ones = jnp.ones((8, count), jnp.bfloat16)
    for head in range(heads):
        hit = jnp.where(reach == offsets_ref[head], 1.0, 0.0).astype(jnp.bfloat16)
        found = dot_nt(ones, hit)[:1]
        slash_ref[head, :, :rows] = jnp.where(found > 0.5, 0.0, DEAD)
        slash_ref[head, :, rows:] = jnp.full((1, rows), DEAD, jnp.float32)


def slash_kernel(rows, heads, offsets_ref, q_ref, slash_ref, qcopy_ref):
    make_slash(offsets_ref, slash_ref, rows, heads)
    qcopy_ref[...] = q_ref[...]


def own_kernel(
    rows, g, group_size,
    q_ref, k_ref, v_ref, band_bias_ref, extra_bias_ref, slash_ref, *refs,
):
    if g:
        gauge_in, *refs = refs
    *sent, acc_ref, sum_ref, shift_ref, gauge_ref, table_ref, held = refs[:-3]
    keys_ref, values_ref, tri_ref = refs[-3:]
    for a, b in zip(sent, held):
        b[...] = a[...]
    t = rows // 2
    tri = lax.broadcasted_iota(jnp.int32, (t, t), 0) >= lax.broadcasted_iota(jnp.int32, (t, t), 1)
    split_keys(k_ref, v_ref, g, rows, keys_ref, values_ref)
    for m in range(2):
        for b in range(2):
            row = band_bias_ref[g, m : m + 1, rows + b * t : rows + (b + 1) * t]
            tri_ref[m, b] = jnp.where(tri, row, DEAD)

    if g:
        gauge_ref[...] = gauge_in[...]
    else:
        gauge_ref[0] = jnp.zeros((8, HEAD_SIZE), jnp.float32)
        gauge_ref[1] = jnp.full((8, HEAD_SIZE), -DEAD, jnp.float32)
    blank = jnp.zeros((t, t), jnp.bfloat16)
    def one_head(h, carry):
        head = g * group_size + h
        at = lanes_of(h)
        t2, t1, t0 = slash_blocks(slash_ref, head, t)
        table_ref[h, :, :t] = t2
        table_ref[h, :, t:] = t1
        for m in range(2):
            q = q_ref[m, :, lanes_of(head)]
            s = dot_nt(q, keys_ref[: (m + 1) * rows]) * SCALE2
            band = s[:, m * rows :]
            row = band_bias_ref[g, m : m + 1, rows : rows + t]
            top = [band[:t, :t] + jnp.maximum(t0, tri_ref[m, 0])]
            low = [
                band[t:, :t] + jnp.maximum(t1, row),
                band[t:, t:] + jnp.maximum(t0, tri_ref[m, 1]),
            ]
            if m == 1:
                more = columns_of(s[:, :rows] + extra_bias_ref[g, :, :rows], 2)
                top = [x[:t] for x in more] + top
                low = [x[t:] for x in more] + low
            top_shift, low_shift = row_max(top), row_max(low)
            p = jnp.concatenate(
                [
                    jnp.concatenate(weights_of(top, top_shift) + [blank], axis=1),
                    jnp.concatenate(weights_of(low, low_shift), axis=1),
                ],
                axis=0,
            )
            o = dot_nn(p, values_ref[: (m + 1) * rows])
            shift = jnp.concatenate([top_shift, low_shift], axis=0)
            acc_ref[m, :, at] = o[:, :HEAD_SIZE]
            sum_ref[m, :, at] = o[:, HEAD_SIZE:]
            shift_ref[m, :, at] = shift
            gauge_ref[0] = jnp.maximum(gauge_ref[0], folded(norms(q), jnp.maximum))
            gauge_ref[1] = jnp.minimum(gauge_ref[1], folded(shift, jnp.minimum))
        return carry

    lax.fori_loop(0, group_size, one_head, 0, unroll=True)


def middle_kernel(
    rows, kv, group_size,
    rank_ref, q_ref, k_ref, v_ref, first_ref, band_bias_ref, extra_bias_ref, remote_bias_ref, *refs,
):
    acc_in, sum_in, shift_in, tables, gauges, acc_ref, sum_ref, shift_ref = (
        refs[i * kv : (i + 1) * kv] for i in range(8)
    )
    keys_ref, values_ref = refs[-2:]
    first_rank = rank_ref[0] == 0
    shut = jnp.where(first_rank, DEAD, 0.0)
    t = rows // 2
    ones = jnp.ones((3 * rows, HEAD_SIZE), jnp.bfloat16)
    key_norm = jnp.zeros((8, HEAD_SIZE), jnp.float32)
    for g in range(kv):
        lanes = slice(g * HEAD_SIZE, (g + 1) * HEAD_SIZE)
        for which, ref, to in ((0, k_ref, keys_ref), (1, v_ref, values_ref)):
            low, high = ref[0, :, lanes], ref[1, :, lanes]
            to[g, :rows, :HEAD_SIZE] = jnp.where(first_rank, low, high)
            to[g, rows : 2 * rows, :HEAD_SIZE] = low
            to[g, 2 * rows :, :HEAD_SIZE] = first_ref[which, :, lanes]
        values_ref[g, :, HEAD_SIZE:] = ones
        for part in range(3):
            k = keys_ref[g, part * rows : (part + 1) * rows]
            key_norm = jnp.maximum(key_norm, folded(norms(k), jnp.maximum))
    fast = in_range(gauges[-1][0], key_norm, gauges[-1][1])

    def scores(g, m, h, q):
        t2, t1 = tables[g][h, :, :t], tables[g][h, :, t:]
        if m == 0:
            t2, t1 = t2 + shut, t1 + shut
        s = dot_nt(q, keys_ref[g, (1 - m) * rows :]) * SCALE2
        band = s[:, :rows]
        row = [band_bias_ref[g, m : m + 1, b * t : (b + 1) * t] for b in range(2)]
        blocks = [
            jnp.concatenate(
                [band[:t, :t] + jnp.maximum(t2, row[0]), band[t:, :t] + row[0]], axis=0
            ),
            jnp.concatenate(
                [
                    band[:t, t:] + jnp.maximum(t1, row[1]),
                    band[t:, t:] + jnp.maximum(t2, row[1]),
                ],
                axis=0,
            ),
        ]
        if m == 1:
            blocks += columns_of(s[:, rows : 2 * rows] + extra_bias_ref[g, :, rows:], 2)
        return blocks + columns_of(s[:, (m + 1) * rows :] + remote_bias_ref[g, m : m + 1, -rows:], 2)

    def merge(g, m, at, blocks, shift, shrink):
        p = jnp.concatenate(weights_of(blocks, shift), axis=1)
        o = dot_nn(p, values_ref[g, (1 - m) * rows :])
        acc, total = acc_in[g][m, :, at], sum_in[g][m, :, at]
        if shrink is not None:
            acc, total = acc * shrink, total * shrink
        acc_ref[g][m, :, at] = acc + o[:, :HEAD_SIZE]
        sum_ref[g][m, :, at] = total + o[:, HEAD_SIZE:]

    @pl.when(fast)
    def _():
        for g in range(kv):

            def one_head(h, carry):
                at, from_q = lanes_of(h), lanes_of(g * group_size + h)
                for m in range(2):
                    shift = shift_in[g][m, :, at]
                    merge(g, m, at, scores(g, m, h, q_ref[m, :, from_q]), shift, None)
                    shift_ref[g][m, :, at] = shift
                return carry

            lax.fori_loop(0, group_size, one_head, 0, unroll=True)

    @pl.when(jnp.logical_not(fast))
    def _():
        for g in range(kv):

            def one_head(h, carry):
                at, from_q = lanes_of(h), lanes_of(g * group_size + h)
                for m in range(2):
                    blocks = scores(g, m, h, q_ref[m, :, from_q])
                    old = shift_in[g][m, :, at]
                    shift = jnp.maximum(old, row_max(blocks))
                    merge(g, m, at, blocks, shift, jnp.exp2(old - shift))
                    shift_ref[g][m, :, at] = shift
                return carry

            lax.fori_loop(0, group_size, one_head, 0)


def far_kernel(rows, g, group_size, count, *refs):
    rank_ref, q_ref, acc_ref, sum_ref, shift_ref, gauge_ref, remote_bias_ref = refs[:7]
    arrived = refs[7 : 7 + count]
    out_hbm, keys_ref, values_ref, out_ref, sems = refs[-5:]
    ones = jnp.ones((rows, HEAD_SIZE), jnp.bfloat16)
    key_norm = jnp.zeros((8, HEAD_SIZE), jnp.float32)
    for i, ref in enumerate(arrived):
        at = slice(i * rows, (i + 1) * rows)
        k = ref[0]
        key_norm = jnp.maximum(key_norm, folded(norms(k), jnp.maximum))
        keys_ref[at, :] = k
        values_ref[at, :HEAD_SIZE] = ref[1]
        values_ref[at, HEAD_SIZE:] = ones
    fast = in_range(gauge_ref[0], key_norm, gauge_ref[1])
    copies = [
        pltpu.make_async_copy(
            out_ref.at[h], out_hbm.at[:, :, lanes_of(g * group_size + h)], sems.at[h]
        )
        for h in range(group_size)
    ]

    def scores(m, q):
        bias = remote_bias_ref[g, m : m + 1, : count * rows]
        s = dot_nt(q, keys_ref[...]) * SCALE2 + bias
        return columns_of(s, count * rows // HEAD_SIZE)

    def finish(h, m, at, blocks, shift, shrink):
        o = dot_nn(jnp.concatenate(weights_of(blocks, shift), axis=1), values_ref[...])
        acc, total = acc_ref[m, :, at], sum_ref[m, :, at]
        if shrink is not None:
            acc, total = acc * shrink, total * shrink
        out = (acc + o[:, :HEAD_SIZE]) / (total + o[:, HEAD_SIZE:])
        out_ref[h, m] = out.astype(jnp.bfloat16)

    def attend(first_half):
        for h in range(group_size):
            at, from_q = lanes_of(h), lanes_of(g * group_size + h)
            if first_half:
                finish(h, 0, at, scores(0, q_ref[0, :, from_q]), shift_ref[0, :, at], None)
            else:
                out_ref[h, 0] = (acc_ref[0, :, at] / sum_ref[0, :, at]).astype(jnp.bfloat16)
            finish(h, 1, at, scores(1, q_ref[1, :, from_q]), shift_ref[1, :, at], None)
            copies[h].start()
        for copy in copies:
            copy.wait()

    sees = rank_ref[0] >= 2
    pl.when(sees)(lambda: attend(True))
    pl.when(jnp.logical_not(sees))(lambda: attend(False))

    @pl.when(jnp.logical_not(fast))
    def _():
        def one_head(h, carry):
            at, from_q = lanes_of(h), lanes_of(g * group_size + h)
            for m in range(2):
                blocks = scores(m, q_ref[m, :, from_q])
                old = shift_ref[m, :, at]
                shift = jnp.maximum(old, row_max(blocks))
                finish(h, m, at, blocks, shift, jnp.exp2(old - shift))
            return carry

        lax.fori_loop(0, group_size, one_head, 0)
        for copy in copies:
            copy.start()
        for copy in copies:
            copy.wait()


def per_device(queries, key_row_table, value_row_table, vertical_cols, slash_offsets):
    n = lax.axis_size("ctx")
    rank = lax.axis_index("ctx").astype(jnp.int32)
    rows = queries.shape[2]
    kv = key_row_table.shape[3] // HEAD_SIZE
    heads = queries.shape[3] // HEAD_SIZE
    group_size = heads // kv
    q, k, v = queries[0], key_row_table[0], value_row_table[0]
    cols = vertical_cols[0]
    offsets = jnp.swapaxes(slash_offsets, 0, 1)
    count = n - 2
    late = n - 3
    per_rank = rows // TILE_COLUMNS
    vmem = pl.BlockSpec(memory_space=pltpu.VMEM)
    smem = pl.BlockSpec(memory_space=pltpu.SMEM)
    hbm = pl.BlockSpec(memory_space=pl.ANY)
    params = pltpu.CompilerParams(vmem_limit_bytes=VMEM_BYTES)
    unit = jax.ShapeDtypeStruct((2, rows, kv * HEAD_SIZE), jnp.bfloat16)
    piece = jax.ShapeDtypeStruct((2, rows, HEAD_SIZE), jnp.bfloat16)
    rank1 = rank[None]

    def shifted(x, d):
        return lax.ppermute(x, "ctx", [(i, (i + d) % n) for i in range(n)])

    k_before, v_before = shifted(k, 1), shifted(v, 1)

    prepared = pl.pallas_call(
        functools.partial(prep_kernel, n, rows, kv),
        out_shape=[piece] * (late * kv)
        + [unit]
        + [
            jax.ShapeDtypeStruct((kv, 2, 2 * rows), jnp.float32),
            jax.ShapeDtypeStruct((kv, 1, 2 * rows), jnp.float32),
            jax.ShapeDtypeStruct((kv, 2, count * rows), jnp.float32),
            jax.ShapeDtypeStruct(k.shape, k.dtype),
            jax.ShapeDtypeStruct(v.shape, v.dtype),
        ],
        in_specs=[smem, smem, vmem, vmem, vmem],
        out_specs=[vmem] * (6 + late * kv),
        scratch_shapes=[
            pltpu.VMEM((2, rows, kv * HEAD_SIZE), jnp.bfloat16),
            pltpu.VMEM((kv, 2 * n * per_rank, TILE_COLUMNS), jnp.float32),
            pltpu.SMEM((kv, n * MAXT), jnp.int32),
            pltpu.SMEM((kv, n), jnp.int32),
        ],
        compiler_params=params,
        name="prep",
    )(rank1, cols, cols, k, v)
    pieces = prepared[: late * kv]
    whole, band_bias, extra_bias, remote_bias, kv_k, kv_v = prepared[late * kv :]
    first = shifted(whole, n - 1)

    state = jax.ShapeDtypeStruct((2, rows, group_size * HEAD_SIZE), jnp.float32)

    def cost(blocks):
        return pl.CostEstimate(
            flops=heads * blocks * rows * rows * HEAD_SIZE * 4,
            bytes_accessed=16_000_000,
            transcendentals=heads * blocks * rows * rows,
        )

    slash, qv = pl.pallas_call(
        functools.partial(slash_kernel, rows, heads),
        out_shape=[
            jax.ShapeDtypeStruct((heads, 1, 2 * rows), jnp.float32),
            jax.ShapeDtypeStruct(q.shape, q.dtype),
        ],
        in_specs=[vmem] * 2,
        out_specs=[vmem] * 2,
        compiler_params=params,
        name="slash",
    )(offsets, q)

    made, arrived = [], []
    for g in range(kv):
        sent = [x[3] for x in made[-1:]] + list(pieces[g::kv])
        *own, held = pl.pallas_call(
            functools.partial(own_kernel, rows, g, group_size),
            out_shape=[
                state,
                state,
                state,
                jax.ShapeDtypeStruct((2, 8, HEAD_SIZE), jnp.float32),
                jax.ShapeDtypeStruct((group_size, rows // 2, rows), jnp.float32),
                [piece] * late,
            ],
            in_specs=[vmem] * (6 + len(sent)),
            out_specs=[vmem] * 5 + [[vmem] * late],
            scratch_shapes=[
                pltpu.VMEM((2 * rows, HEAD_SIZE), jnp.bfloat16),
                pltpu.VMEM((2 * rows, 2 * HEAD_SIZE), jnp.bfloat16),
                pltpu.VMEM((2, 2, rows // 2, rows // 2), jnp.float32),
            ],
            compiler_params=params,
            cost_estimate=cost(2),
            name="own",
        )(qv, kv_k, kv_v, band_bias, extra_bias, slash, *sent)
        made.append(own)
        arrived.append([shifted(x, i + 2) for i, x in enumerate(held)])
    accs, totals, shifts, gauges, tables = zip(*made)

    states = pl.pallas_call(
        functools.partial(middle_kernel, rows, kv, group_size),
        out_shape=[state] * (3 * kv),
        in_specs=[smem] + [vmem] * (7 + 5 * kv),
        out_specs=[vmem] * (3 * kv),
        scratch_shapes=[
            pltpu.VMEM((kv, 3 * rows, HEAD_SIZE), jnp.bfloat16),
            pltpu.VMEM((kv, 3 * rows, 2 * HEAD_SIZE), jnp.bfloat16),
        ],
        input_output_aliases={8 + i: i for i in range(3 * kv)},
        compiler_params=params,
        cost_estimate=cost(5),
        name="middle",
    )(
        rank1, qv, k_before, v_before, first, band_bias, extra_bias, remote_bias,
        *accs, *totals, *shifts, *tables, *gauges,
    )

    out = []
    for g in range(kv):
        out = [
            pl.pallas_call(
                functools.partial(far_kernel, rows, g, group_size, late),
                out_shape=jax.ShapeDtypeStruct(q.shape, jnp.bfloat16),
                in_specs=[smem] + [vmem] * (6 + late) + [hbm] * len(out),
                out_specs=hbm,
                scratch_shapes=[
                    pltpu.VMEM((late * rows, HEAD_SIZE), jnp.bfloat16),
                    pltpu.VMEM((late * rows, 2 * HEAD_SIZE), jnp.bfloat16),
                    pltpu.VMEM((group_size, 2, rows, HEAD_SIZE), jnp.bfloat16),
                    pltpu.SemaphoreType.DMA((group_size,)),
                ],
                input_output_aliases={7 + late: 0} if out else {},
                compiler_params=params,
                cost_estimate=cost(late),
                name="far",
            )(rank1, qv, *states[g::kv], gauges[g], remote_bias, *arrived[g], *out)
        ]
    return out[0][None]


def solution(mesh):
    in_specs = (
        P("section", None, ("groups", "ctx"), "head"),
        P("section", None, ("groups", "ctx"), "head"),
        P("section", None, ("groups", "ctx"), "head"),
        P("section", "head", "groups"),
        P("section", "head", "groups"),
    )
    out_specs = P("section", None, ("groups", "ctx"), "head")
    return jax.shard_map(
        per_device, mesh=mesh, in_specs=in_specs, out_specs=out_specs, check_vma=False
    )
```

```python
import functools
import math

import jax
import jax.numpy as jnp
from jax import lax
from jax.experimental import pallas as pl
from jax.experimental.pallas import tpu as pltpu
from jax.sharding import PartitionSpec as P

HEAD_SIZE = 128
TILE_COLUMNS = 128
MAXT = 2
DEAD = -1e30
SCALE2 = math.log2(math.e) / math.sqrt(HEAD_SIZE)
VMEM_BYTES = 24 * 1024 * 1024
REACH = 100.0


def dot_nt(a, b):
    return lax.dot_general(a, b, (((1,), (1,)), ((), ())), preferred_element_type=jnp.float32)


def dot_nn(a, b):
    return lax.dot_general(a, b, (((1,), (0,)), ((), ())), preferred_element_type=jnp.float32)


def prep_kernel(n, rows, kv, rank_ref, cols_smem, cols_ref, k_ref, v_ref, *outs):
    parts = (n - 3) * kv
    split_refs, whole_ref = outs[:parts], outs[parts]
    band_bias_ref, extra_bias_ref, remote_bias_ref, kcopy_ref, vcopy_ref = outs[parts + 1 : parts + 6]
    outbox_ref, marks_ref, slot_ref, count_ref = outs[parts + 6 :]
    kcopy_ref[...] = k_ref[...]
    vcopy_ref[...] = v_ref[...]
    rank = rank_ref[0]
    half_len = rows * n
    tiles = cols_ref.shape[1] // TILE_COLUMNS
    per_rank = rows // TILE_COLUMNS

    for g in range(kv):
        for s in range(n):
            count_ref[g, s] = 0
            for slot in range(MAXT):
                slot_ref[g, s * MAXT + slot] = -1
        for t in range(tiles):
            owner = cols_smem[g, t * TILE_COLUMNS] % half_len // rows
            seen = count_ref[g, owner]
            slot_ref[g, owner * MAXT + seen] = t
            count_ref[g, owner] = seen + 1

    for g in range(kv):
        lanes = slice(g * HEAD_SIZE, (g + 1) * HEAD_SIZE)
        for slot in range(MAXT):
            tile = jnp.maximum(slot_ref[g, rank * MAXT + slot], 0)
            start = pl.multiple_of(tile * TILE_COLUMNS, TILE_COLUMNS)
            half = cols_smem[g, start] // half_len
            within = cols_ref[pl.ds(g, 1), pl.ds(start, TILE_COLUMNS)] % rows
            hit = lax.broadcasted_iota(jnp.int32, (rows, TILE_COLUMNS), 0) == within
            pick = jnp.where(hit, 1.0, 0.0).astype(jnp.bfloat16)
            for which, ref in enumerate((k_ref, v_ref)):
                source = ref[pl.ds(half, 1), :, lanes][0]
                got = lax.dot_general(
                    pick, source, (((0,), (0,)), ((), ())), preferred_element_type=jnp.float32
                )
                outbox_ref[which, slot * TILE_COLUMNS : (slot + 1) * TILE_COLUMNS, lanes] = (
                    got.astype(jnp.bfloat16)
                )
    for i in range(n - 2):
        later = rank + i + 2 < n
        refs = [whole_ref] if i == n - 3 else split_refs[i * kv : (i + 1) * kv]
        wide = kv * HEAD_SIZE // len(refs)

        @pl.when(later)
        def _():
            for j, ref in enumerate(refs):
                ref[...] = outbox_ref[:, :, j * wide : (j + 1) * wide]

        @pl.when(jnp.logical_not(later))
        def _():
            for j, ref in enumerate(refs):
                ref[0] = k_ref[0, :, j * wide : (j + 1) * wide]
                ref[1] = v_ref[0, :, j * wide : (j + 1) * wide]

    blocks = 2 * n * per_rank
    dead_row = jnp.full((1, rows), DEAD, jnp.float32)
    for g in range(kv):
        cols = cols_ref[g : g + 1, :]
        high = lax.broadcasted_iota(jnp.int32, (blocks, cols.shape[1]), 0) == cols // TILE_COLUMNS
        low = lax.broadcasted_iota(jnp.int32, (TILE_COLUMNS, cols.shape[1]), 0) == cols % TILE_COLUMNS
        count = dot_nt(
            jnp.where(high, 1.0, 0.0).astype(jnp.bfloat16),
            jnp.where(low, 1.0, 0.0).astype(jnp.bfloat16),
        )
        marks_ref[g] = jnp.where(count > 0.5, 0.0, DEAD)

        def marks_of(half, s):
            first = (half * n + s) * per_rank
            return jnp.concatenate(
                [marks_ref[g, pl.ds(first + i, 1), :] for i in range(per_rank)], axis=1
            )

        first_rank = rank == 0
        before = jnp.where(first_rank, n - 1, rank - 1)
        before_low = marks_of(0, before)
        own_low = marks_of(0, rank)
        own_high = marks_of(1, rank)
        before_high = marks_of(jnp.where(first_rank, 0, 1), before)
        band_bias_ref[g, 0:1, :rows] = jnp.where(first_rank, dead_row, before_low)
        band_bias_ref[g, 0:1, rows:] = own_low
        band_bias_ref[g, 1:2, :rows] = before_high
        band_bias_ref[g, 1:2, rows:] = own_high
        extra_bias_ref[g, 0:1, :rows] = own_low
        extra_bias_ref[g, 0:1, rows:] = jnp.where(first_rank, dead_row, before_low)
        for i in range(n - 2):
            d = i + 2
            earlier = rank >= d
            s = jnp.where(earlier, rank - d, rank - d + n)
            raw = marks_of(0, s)
            for slot in range(MAXT):
                tile = slot_ref[g, s * MAXT + slot]
                half = cols_smem[g, jnp.maximum(tile, 0) * TILE_COLUMNS] // half_len
                live = tile >= 0
                high_value = jnp.where(live, 0.0, DEAD)
                low_value = jnp.where(live & (half == 0) & earlier, 0.0, DEAD)
                span = slice(i * rows + slot * TILE_COLUMNS, i * rows + (slot + 1) * TILE_COLUMNS)
                part = slice(slot * TILE_COLUMNS, (slot + 1) * TILE_COLUMNS)
                remote_bias_ref[g, 0:1, span] = jnp.full((1, TILE_COLUMNS), low_value, jnp.float32)
                remote_bias_ref[g, 1:2, span] = jnp.where(
                    earlier, jnp.full((1, TILE_COLUMNS), high_value, jnp.float32), raw[:, part]
                )


def lane_sums(x):
    ones = jnp.ones((x.shape[1], HEAD_SIZE), jnp.bfloat16)
    return dot_nn(x.astype(jnp.bfloat16), ones)


def folded(x, op):
    while x.shape[0] > 8:
        half = x.shape[0] // 2
        x = op(x[:half], x[half:])
    return x


def norms(x):
    x = x.astype(jnp.float32)
    return lane_sums(x * x)


def in_range(query_norm, key_norm, lowest):
    bound = jnp.sqrt(jnp.max(query_norm)) * jnp.sqrt(jnp.max(key_norm)) * (1.02 * SCALE2)
    return bound - jnp.min(lowest) <= REACH


def lanes_of(head):
    return pl.ds(pl.multiple_of(head * HEAD_SIZE, HEAD_SIZE), HEAD_SIZE)


def split_keys(k_ref, v_ref, g, rows, keys_ref, values_ref):
    lanes = slice(g * HEAD_SIZE, (g + 1) * HEAD_SIZE)
    for ref, to in ((k_ref, keys_ref), (v_ref, values_ref)):
        to[:rows, :HEAD_SIZE] = ref[0, :, lanes]
        to[rows:, :HEAD_SIZE] = ref[1, :, lanes]
    values_ref[:, HEAD_SIZE:] = jnp.ones((2 * rows, HEAD_SIZE), jnp.bfloat16)


def slash_blocks(slash_ref, head, t):
    base = jnp.broadcast_to(slash_ref[head], (t, 4 * t))
    rolled = pltpu.roll(base, 1, 1, stride=1, stride_axis=0)
    return rolled[:, :t], rolled[:, t : 2 * t], rolled[:, 2 * t : 3 * t]


def weights_of(blocks, shift):
    return [jnp.exp2(x - shift).astype(jnp.bfloat16) for x in blocks]


def row_max(blocks):
    x = functools.reduce(jnp.maximum, blocks)
    return jnp.broadcast_to(jnp.max(x, axis=1, keepdims=True), x.shape)


def columns_of(s, count):
    return [s[:, b * HEAD_SIZE : (b + 1) * HEAD_SIZE] for b in range(count)]


def make_slash(offsets_ref, slash_ref, rows, heads):
    count = offsets_ref.shape[2]
    reach = rows - 1 - lax.broadcasted_iota(jnp.int32, (rows, count), 0)
    ones = jnp.ones((8, count), jnp.bfloat16)
    for head in range(heads):
        hit = jnp.where(reach == offsets_ref[head], 1.0, 0.0).astype(jnp.bfloat16)
        found = dot_nt(ones, hit)[:1]
        slash_ref[head, :, :rows] = jnp.where(found > 0.5, 0.0, DEAD)
        slash_ref[head, :, rows:] = jnp.full((1, rows), DEAD, jnp.float32)


def slash_kernel(rows, heads, offsets_ref, q_ref, slash_ref, qcopy_ref):
    make_slash(offsets_ref, slash_ref, rows, heads)
    qcopy_ref[...] = q_ref[...]


def own_kernel(
    rows, g, group_size,
    q_ref, k_ref, v_ref, band_bias_ref, extra_bias_ref, slash_ref, *refs,
):
    if g:
        gauge_in, *refs = refs
    *sent, acc_ref, sum_ref, shift_ref, gauge_ref, table_ref, held = refs[:-3]
    keys_ref, values_ref, tri_ref = refs[-3:]
    for a, b in zip(sent, held):
        b[...] = a[...]
    t = rows // 2
    tri = lax.broadcasted_iota(jnp.int32, (t, t), 0) >= lax.broadcasted_iota(jnp.int32, (t, t), 1)
    split_keys(k_ref, v_ref, g, rows, keys_ref, values_ref)
    for m in range(2):
        for b in range(2):
            row = band_bias_ref[g, m : m + 1, rows + b * t : rows + (b + 1) * t]
            tri_ref[m, b] = jnp.where(tri, row, DEAD)

    if g:
        gauge_ref[...] = gauge_in[...]
    else:
        gauge_ref[0] = jnp.zeros((8, HEAD_SIZE), jnp.float32)
        gauge_ref[1] = jnp.full((8, HEAD_SIZE), -DEAD, jnp.float32)
    blank = jnp.zeros((t, t), jnp.bfloat16)
    def one_head(h, carry):
        head = g * group_size + h
        at = lanes_of(h)
        t2, t1, t0 = slash_blocks(slash_ref, head, t)
        table_ref[h, :, :t] = t2
        table_ref[h, :, t:] = t1
        for m in range(2):
            q = q_ref[m, :, lanes_of(head)]
            s = dot_nt(q, keys_ref[: (m + 1) * rows]) * SCALE2
            band = s[:, m * rows :]
            row = band_bias_ref[g, m : m + 1, rows : rows + t]
            top = [band[:t, :t] + jnp.maximum(t0, tri_ref[m, 0])]
            low = [
                band[t:, :t] + jnp.maximum(t1, row),
                band[t:, t:] + jnp.maximum(t0, tri_ref[m, 1]),
            ]
            if m == 1:
                more = columns_of(s[:, :rows] + extra_bias_ref[g, :, :rows], 2)
                top = [x[:t] for x in more] + top
                low = [x[t:] for x in more] + low
            top_shift, low_shift = row_max(top), row_max(low)
            p = jnp.concatenate(
                [
                    jnp.concatenate(weights_of(top, top_shift) + [blank], axis=1),
                    jnp.concatenate(weights_of(low, low_shift), axis=1),
                ],
                axis=0,
            )
            o = dot_nn(p, values_ref[: (m + 1) * rows])
            shift = jnp.concatenate([top_shift, low_shift], axis=0)
            acc_ref[m, :, at] = o[:, :HEAD_SIZE]
            sum_ref[m, :, at] = o[:, HEAD_SIZE:]
            shift_ref[m, :, at] = shift
            gauge_ref[0] = jnp.maximum(gauge_ref[0], folded(norms(q), jnp.maximum))
            gauge_ref[1] = jnp.minimum(gauge_ref[1], folded(shift, jnp.minimum))
        return carry

    lax.fori_loop(0, group_size, one_head, 0, unroll=True)


def middle_kernel(
    rows, kv, group_size,
    rank_ref, q_ref, k_ref, v_ref, first_ref, band_bias_ref, extra_bias_ref, remote_bias_ref, *refs,
):
    acc_in, sum_in, shift_in, tables, gauges, acc_ref, sum_ref, shift_ref = (
        refs[i * kv : (i + 1) * kv] for i in range(8)
    )
    keys_ref, values_ref = refs[-2:]
    first_rank = rank_ref[0] == 0
    shut = jnp.where(first_rank, DEAD, 0.0)
    t = rows // 2
    ones = jnp.ones((3 * rows, HEAD_SIZE), jnp.bfloat16)
    key_norm = jnp.zeros((8, HEAD_SIZE), jnp.float32)
    for g in range(kv):
        lanes = slice(g * HEAD_SIZE, (g + 1) * HEAD_SIZE)
        for which, ref, to in ((0, k_ref, keys_ref), (1, v_ref, values_ref)):
            low, high = ref[0, :, lanes], ref[1, :, lanes]
            to[g, :rows, :HEAD_SIZE] = jnp.where(first_rank, low, high)
            to[g, rows : 2 * rows, :HEAD_SIZE] = low
            to[g, 2 * rows :, :HEAD_SIZE] = first_ref[which, :, lanes]
        values_ref[g, :, HEAD_SIZE:] = ones
        for part in range(3):
            k = keys_ref[g, part * rows : (part + 1) * rows]
            key_norm = jnp.maximum(key_norm, folded(norms(k), jnp.maximum))
    fast = in_range(gauges[-1][0], key_norm, gauges[-1][1])

    def scores(g, m, h, q):
        t2, t1 = tables[g][h, :, :t], tables[g][h, :, t:]
        if m == 0:
            t2, t1 = t2 + shut, t1 + shut
        s = dot_nt(q, keys_ref[g, (1 - m) * rows :]) * SCALE2
        band = s[:, :rows]
        row = [band_bias_ref[g, m : m + 1, b * t : (b + 1) * t] for b in range(2)]
        blocks = [
            jnp.concatenate(
                [band[:t, :t] + jnp.maximum(t2, row[0]), band[t:, :t] + row[0]], axis=0
            ),
            jnp.concatenate(
                [
                    band[:t, t:] + jnp.maximum(t1, row[1]),
                    band[t:, t:] + jnp.maximum(t2, row[1]),
                ],
                axis=0,
            ),
        ]
        if m == 1:
            blocks += columns_of(s[:, rows : 2 * rows] + extra_bias_ref[g, :, rows:], 2)
        return blocks + columns_of(s[:, (m + 1) * rows :] + remote_bias_ref[g, m : m + 1, -rows:], 2)

    def merge(g, m, at, blocks, shift, shrink):
        p = jnp.concatenate(weights_of(blocks, shift), axis=1)
        o = dot_nn(p, values_ref[g, (1 - m) * rows :])
        acc, total = acc_in[g][m, :, at], sum_in[g][m, :, at]
        if shrink is not None:
            acc, total = acc * shrink, total * shrink
        acc_ref[g][m, :, at] = acc + o[:, :HEAD_SIZE]
        sum_ref[g][m, :, at] = total + o[:, HEAD_SIZE:]

    @pl.when(fast)
    def _():
        for g in range(kv):

            def one_head(h, carry):
                at, from_q = lanes_of(h), lanes_of(g * group_size + h)
                for m in range(2):
                    shift = shift_in[g][m, :, at]
                    merge(g, m, at, scores(g, m, h, q_ref[m, :, from_q]), shift, None)
                    shift_ref[g][m, :, at] = shift
                return carry

            lax.fori_loop(0, group_size, one_head, 0, unroll=True)

    @pl.when(jnp.logical_not(fast))
    def _():
        for g in range(kv):

            def one_head(h, carry):
                at, from_q = lanes_of(h), lanes_of(g * group_size + h)
                for m in range(2):
                    blocks = scores(g, m, h, q_ref[m, :, from_q])
                    old = shift_in[g][m, :, at]
                    shift = jnp.maximum(old, row_max(blocks))
                    merge(g, m, at, blocks, shift, jnp.exp2(old - shift))
                    shift_ref[g][m, :, at] = shift
                return carry

            lax.fori_loop(0, group_size, one_head, 0)


def far_kernel(rows, g, group_size, count, *refs):
    rank_ref, q_ref, acc_ref, sum_ref, shift_ref, gauge_ref, remote_bias_ref = refs[:7]
    arrived = refs[7 : 7 + count]
    out_hbm, keys_ref, values_ref, out_ref, sems = refs[-5:]
    ones = jnp.ones((rows, HEAD_SIZE), jnp.bfloat16)
    key_norm = jnp.zeros((8, HEAD_SIZE), jnp.float32)
    for i, ref in enumerate(arrived):
        at = slice(i * rows, (i + 1) * rows)
        k = ref[0]
        key_norm = jnp.maximum(key_norm, folded(norms(k), jnp.maximum))
        keys_ref[at, :] = k
        values_ref[at, :HEAD_SIZE] = ref[1]
        values_ref[at, HEAD_SIZE:] = ones
    fast = in_range(gauge_ref[0], key_norm, gauge_ref[1])
    copies = [
        pltpu.make_async_copy(
            out_ref.at[h, m], out_hbm.at[m, :, lanes_of(g * group_size + h)], sems.at[2 * h + m]
        )
        for h in range(group_size)
        for m in range(2)
    ]

    def scores(m, q):
        bias = remote_bias_ref[g, m : m + 1, : count * rows]
        s = dot_nt(q, keys_ref[...]) * SCALE2 + bias
        return columns_of(s, count * rows // HEAD_SIZE)

    def finish(h, m, at, blocks, shift, shrink):
        o = dot_nn(jnp.concatenate(weights_of(blocks, shift), axis=1), values_ref[...])
        acc, total = acc_ref[m, :, at], sum_ref[m, :, at]
        if shrink is not None:
            acc, total = acc * shrink, total * shrink
        out = (acc + o[:, :HEAD_SIZE]) / (total + o[:, HEAD_SIZE:])
        out_ref[h, m] = out.astype(jnp.bfloat16)

    def attend(first_half):
        if not first_half:
            for h in range(group_size):
                at = lanes_of(h)
                out_ref[h, 0] = (acc_ref[0, :, at] / sum_ref[0, :, at]).astype(jnp.bfloat16)
                copies[2 * h].start()
        for h in range(group_size):
            at, from_q = lanes_of(h), lanes_of(g * group_size + h)
            if first_half:
                finish(h, 0, at, scores(0, q_ref[0, :, from_q]), shift_ref[0, :, at], None)
                copies[2 * h].start()
            finish(h, 1, at, scores(1, q_ref[1, :, from_q]), shift_ref[1, :, at], None)
            copies[2 * h + 1].start()
        for copy in copies:
            copy.wait()

    sees = rank_ref[0] >= 2
    pl.when(sees)(lambda: attend(True))
    pl.when(jnp.logical_not(sees))(lambda: attend(False))

    @pl.when(jnp.logical_not(fast))
    def _():
        def one_head(h, carry):
            at, from_q = lanes_of(h), lanes_of(g * group_size + h)
            for m in range(2):
                blocks = scores(m, q_ref[m, :, from_q])
                old = shift_ref[m, :, at]
                shift = jnp.maximum(old, row_max(blocks))
                finish(h, m, at, blocks, shift, jnp.exp2(old - shift))
            return carry

        lax.fori_loop(0, group_size, one_head, 0)
        for copy in copies:
            copy.start()
        for copy in copies:
            copy.wait()


def per_device(queries, key_row_table, value_row_table, vertical_cols, slash_offsets):
    n = lax.axis_size("ctx")
    rank = lax.axis_index("ctx").astype(jnp.int32)
    rows = queries.shape[2]
    kv = key_row_table.shape[3] // HEAD_SIZE
    heads = queries.shape[3] // HEAD_SIZE
    group_size = heads // kv
    q, k, v = queries[0], key_row_table[0], value_row_table[0]
    cols = vertical_cols[0]
    offsets = jnp.swapaxes(slash_offsets, 0, 1)
    count = n - 2
    late = n - 3
    per_rank = rows // TILE_COLUMNS
    vmem = pl.BlockSpec(memory_space=pltpu.VMEM)
    smem = pl.BlockSpec(memory_space=pltpu.SMEM)
    hbm = pl.BlockSpec(memory_space=pl.ANY)
    params = pltpu.CompilerParams(vmem_limit_bytes=VMEM_BYTES)
    unit = jax.ShapeDtypeStruct((2, rows, kv * HEAD_SIZE), jnp.bfloat16)
    piece = jax.ShapeDtypeStruct((2, rows, HEAD_SIZE), jnp.bfloat16)
    rank1 = rank[None]

    def shifted(x, d):
        return lax.ppermute(x, "ctx", [(i, (i + d) % n) for i in range(n)])

    k_before, v_before = shifted(k, 1), shifted(v, 1)

    prepared = pl.pallas_call(
        functools.partial(prep_kernel, n, rows, kv),
        out_shape=[piece] * (late * kv)
        + [unit]
        + [
            jax.ShapeDtypeStruct((kv, 2, 2 * rows), jnp.float32),
            jax.ShapeDtypeStruct((kv, 1, 2 * rows), jnp.float32),
            jax.ShapeDtypeStruct((kv, 2, count * rows), jnp.float32),
            jax.ShapeDtypeStruct(k.shape, k.dtype),
            jax.ShapeDtypeStruct(v.shape, v.dtype),
        ],
        in_specs=[smem, smem, vmem, vmem, vmem],
        out_specs=[vmem] * (6 + late * kv),
        scratch_shapes=[
            pltpu.VMEM((2, rows, kv * HEAD_SIZE), jnp.bfloat16),
            pltpu.VMEM((kv, 2 * n * per_rank, TILE_COLUMNS), jnp.float32),
            pltpu.SMEM((kv, n * MAXT), jnp.int32),
            pltpu.SMEM((kv, n), jnp.int32),
        ],
        compiler_params=params,
        name="prep",
    )(rank1, cols, cols, k, v)
    pieces = prepared[: late * kv]
    whole, band_bias, extra_bias, remote_bias, kv_k, kv_v = prepared[late * kv :]
    first = shifted(whole, n - 1)

    state = jax.ShapeDtypeStruct((2, rows, group_size * HEAD_SIZE), jnp.float32)

    def cost(blocks):
        return pl.CostEstimate(
            flops=heads * blocks * rows * rows * HEAD_SIZE * 4,
            bytes_accessed=16_000_000,
            transcendentals=heads * blocks * rows * rows,
        )

    slash, qv = pl.pallas_call(
        functools.partial(slash_kernel, rows, heads),
        out_shape=[
            jax.ShapeDtypeStruct((heads, 1, 2 * rows), jnp.float32),
            jax.ShapeDtypeStruct(q.shape, q.dtype),
        ],
        in_specs=[vmem] * 2,
        out_specs=[vmem] * 2,
        compiler_params=params,
        name="slash",
    )(offsets, q)

    made, arrived = [], []
    for g in range(kv):
        sent = [x[3] for x in made[-1:]] + list(pieces[g::kv])
        *own, held = pl.pallas_call(
            functools.partial(own_kernel, rows, g, group_size),
            out_shape=[
                state,
                state,
                state,
                jax.ShapeDtypeStruct((2, 8, HEAD_SIZE), jnp.float32),
                jax.ShapeDtypeStruct((group_size, rows // 2, rows), jnp.float32),
                [piece] * late,
            ],
            in_specs=[vmem] * (6 + len(sent)),
            out_specs=[vmem] * 5 + [[vmem] * late],
            scratch_shapes=[
                pltpu.VMEM((2 * rows, HEAD_SIZE), jnp.bfloat16),
                pltpu.VMEM((2 * rows, 2 * HEAD_SIZE), jnp.bfloat16),
                pltpu.VMEM((2, 2, rows // 2, rows // 2), jnp.float32),
            ],
            compiler_params=params,
            cost_estimate=cost(2),
            name="own",
        )(qv, kv_k, kv_v, band_bias, extra_bias, slash, *sent)
        made.append(own)
        arrived.append([shifted(x, i + 2) for i, x in enumerate(held)])
    accs, totals, shifts, gauges, tables = zip(*made)

    states = pl.pallas_call(
        functools.partial(middle_kernel, rows, kv, group_size),
        out_shape=[state] * (3 * kv),
        in_specs=[smem] + [vmem] * (7 + 5 * kv),
        out_specs=[vmem] * (3 * kv),
        scratch_shapes=[
            pltpu.VMEM((kv, 3 * rows, HEAD_SIZE), jnp.bfloat16),
            pltpu.VMEM((kv, 3 * rows, 2 * HEAD_SIZE), jnp.bfloat16),
        ],
        input_output_aliases={8 + i: i for i in range(3 * kv)},
        compiler_params=params,
        cost_estimate=cost(5),
        name="middle",
    )(
        rank1, qv, k_before, v_before, first, band_bias, extra_bias, remote_bias,
        *accs, *totals, *shifts, *tables, *gauges,
    )

    out = []
    for g in range(kv):
        out = [
            pl.pallas_call(
                functools.partial(far_kernel, rows, g, group_size, late),
                out_shape=jax.ShapeDtypeStruct(q.shape, jnp.bfloat16),
                in_specs=[smem] + [vmem] * (6 + late) + [hbm] * len(out),
                out_specs=hbm,
                scratch_shapes=[
                    pltpu.VMEM((late * rows, HEAD_SIZE), jnp.bfloat16),
                    pltpu.VMEM((late * rows, 2 * HEAD_SIZE), jnp.bfloat16),
                    pltpu.VMEM((group_size, 2, rows, HEAD_SIZE), jnp.bfloat16),
                    pltpu.SemaphoreType.DMA((2 * group_size,)),
                ],
                input_output_aliases={7 + late: 0} if out else {},
                compiler_params=params,
                cost_estimate=cost(late),
                name="far",
            )(rank1, qv, *states[g::kv], gauges[g], remote_bias, *arrived[g], *out)
        ]
    return out[0][None]


def solution(mesh):
    in_specs = (
        P("section", None, ("groups", "ctx"), "head"),
        P("section", None, ("groups", "ctx"), "head"),
        P("section", None, ("groups", "ctx"), "head"),
        P("section", "head", "groups"),
        P("section", "head", "groups"),
    )
    out_specs = P("section", None, ("groups", "ctx"), "head")
    return jax.shard_map(
        per_device, mesh=mesh, in_specs=in_specs, out_specs=out_specs, check_vma=False
    )
```
